32 devices in a mesh: slab: 8 (over z, y), col: 4 (over x, core).
Axes of the slice: x: 2, y: 2, z: 4, core: 2. Of those that a mesh axis runs over, the one named last changes fastest.
Arguments:
- input_map: float32 [64, 16, 192, 128], P('col', 'slab'), may hold values from -24 to 24
- output_map: float32 [64, 16, 192, 128], P('col', 'slab'), may hold values from -24 to 24
- region_ids: int32 [16, 192, 128], P('slab'), may hold values from 0 to 7
- region_cond: float32 [8], replicated, may hold values from 0.3 to 3
- shift_ids: int32 [2], replicated, may hold values from 0 to 7
Outputs:
- ctrl_factor: float32 [2, 64, 16, 192, 128], P(None, None, 'slab', 'col')
- obsv_factor: float32 [2, 64, 16, 192, 128], P(None, None, 'slab', 'col')
- cross_gram: float32 [128, 128], P('slab', 'col')
The draws below stay inside these ranges and needn't reach their ends.
All inputs are finite; a program needn't handle non-finite values.
Results may differ from the reference program's by a relative error of at most 0.000098.
Values sent between devices are 32-bit elements; how exact they have to be, the bound alone decides.
No kernel may reach another device: no remote copies, remote signals or barrier semaphores. Data moves between devices by JAX's collectives and lax.ppermute only.
A program may use at most 192 MiB of HBM per device.

```python
import math
import jax
import jax.numpy as jnp
from jax import lax

K = 64
ADI = 2
STEPS = 3
NY = 192
NZ = 128
REGIONS = 8
SHIFTS = 8
NX = 16
NCELLS = 393216


def with_ends(entries, own_key, smallest, top_value):
    index_at = [jax.random.randint(jax.random.fold_in(own_key, axis), (), 0, length) for axis, length in enumerate(entries.shape)]
    main_axis = entries.shape.index(max(entries.shape))
    next_to = index_at[:main_axis] + [(index_at[main_axis] + 1) % entries.shape[main_axis]] + index_at[main_axis + 1:]
    return entries.at[tuple(index_at)].set(smallest).at[tuple(next_to)].set(top_value)


def shard_levels(own_key, dims, shards, least, high):
    def one(axis_at, parts):
        heights = jax.random.uniform(jax.random.fold_in(jax.random.fold_in(own_key, 6), axis_at), (parts,), jnp.float32, least / len(shards), high / len(shards))
        return jnp.repeat(jnp.exp(heights), dims[axis_at] // parts).reshape((-1,) + (1,) * (len(dims) - axis_at - 1))

    loudness = one(*shards[0])
    for cut in shards[1:]:
        loudness = loudness * one(*cut)
    return loudness


def normal_values(own_key, shape, scale, limit, cuts=(), held_as=jnp.bfloat16):
    values = jax.random.normal(own_key, shape, jnp.float32) * scale
    if len(cuts) > 0:
        values = shard_levels(own_key, shape, cuts, -0.22, 0.18) * values
    return jnp.clip(values, min=-limit, max=limit).astype(held_as)


def setup_inputs(seed: int = 0) -> dict:
    splits = jax.random.split(jax.random.key(seed), 6)
    input_map = normal_values(splits[0], (K, NX, NY, NZ), 4.0, 24.0, ((0, 4), (1, 8)), jnp.float32)
    output_map = normal_values(splits[1], (K, NX, NY, NZ), 4.0, 24.0, ((0, 4), (1, 8)), jnp.float32)
    region_ids = with_ends(jax.random.randint(splits[2], (NX, NY, NZ), 0, REGIONS), jax.random.fold_in(splits[2], 1), 0, REGIONS - 1).astype(jnp.int32)
    region_cond = jnp.clip(jnp.exp(jax.random.uniform(splits[3], (REGIONS,), jnp.float32, math.log(0.3), math.log(3.0))), 0.3, 3.0)
    shift_ids = jax.random.randint(splits[4], (ADI,), 0, SHIFTS).astype(jnp.int32)
    return dict(input_map=input_map, output_map=output_map, region_ids=region_ids, region_cond=region_cond, shift_ids=shift_ids)


def lookup(region_ids, region_cond):
    summed = jnp.zeros(region_ids.shape, jnp.float32)
    for region in range(region_cond.shape[0]):
        summed = summed + jnp.where(region_ids == region, region_cond[region], jnp.float32(0.0))
    return summed

def conduction(field_in, cond_ext):
    centre = field_in[:, 1:-1]
    cond_mid = cond_ext[1:-1]
    summed = 0.5 * (cond_mid + cond_ext[2:]) * (centre - field_in[:, 2:])
    summed = summed + 0.5 * (cond_mid + cond_ext[:-2]) * (centre - field_in[:, :-2])
    cond_y = jnp.pad(cond_mid, ((0, 0), (1, 1), (0, 0)))
    field_y = jnp.pad(centre, ((0, 0), (0, 0), (1, 1), (0, 0)))
    summed = summed + 0.5 * (cond_mid + cond_y[:, 2:]) * (centre - field_y[:, :, 2:])
    summed = summed + 0.5 * (cond_mid + cond_y[:, :-2]) * (centre - field_y[:, :, :-2])
    cond_z = jnp.pad(cond_mid, ((0, 0), (0, 0), (1, 1)))
    field_z = jnp.pad(centre, ((0, 0), (0, 0), (0, 0), (1, 1)))
    summed = summed + 0.5 * (cond_mid + cond_z[:, :, 2:]) * (centre - field_z[:, :, :, 2:])
    summed = summed + 0.5 * (cond_mid + cond_z[:, :, :-2]) * (centre - field_z[:, :, :, :-2])
    return summed

def bounds(shift_val, cond_max):
    low_eig = shift_val
    high_eig = shift_val + 12.0 * cond_max
    mid_eig = 0.5 * (high_eig + low_eig)
    half_span = 0.5 * (high_eig - low_eig)
    return (mid_eig, half_span, mid_eig / half_span)

def reference(input_map, output_map, region_ids, region_cond, shift_ids):
    cond_cells = lookup(region_ids, region_cond)
    cond_pad = jnp.pad(cond_cells, ((1, 1), (0, 0), (0, 0)))
    cond_max = jnp.max(region_cond)
    shifts = 0.25 * jnp.exp2(shift_ids.astype(jnp.float32))

    def chebyshev(right_side, shift_val):
        mid_eig, half_span, ratio_eig = bounds(shift_val, cond_max)
        rho_now = 1.0 / ratio_eig
        solution = jnp.zeros_like(right_side)
        residual = right_side
        direction = right_side / mid_eig
        for sweep_idx in range(STEPS):
            solution = solution + direction
            if sweep_idx < STEPS - 1:
                padded = jnp.pad(direction, ((0, 0), (1, 1), (0, 0), (0, 0)))
                applied = conduction(padded, cond_pad) + shift_val * direction
                residual = residual - applied
                rho_next = 1.0 / (2.0 * ratio_eig - rho_now)
                direction = rho_next * rho_now * direction + 2.0 * rho_next / half_span * residual
                rho_now = rho_next
        return solution
    stacked = jnp.concatenate([input_map, output_map], 0)
    factors = []
    current = stacked
    for segment_idx in range(ADI):
        shift_val = shifts[segment_idx]
        if segment_idx == 0:
            current = chebyshev(stacked, shift_val)
        else:
            current = current - (shifts[segment_idx - 1] + shift_val) * chebyshev(current, shift_val)
        factors.append(jnp.sqrt(2.0 * shift_val) * current)
    ctrl_factor = jnp.stack([factor_part[:K] for factor_part in factors])
    obsv_factor = jnp.stack([factor_part[K:] for factor_part in factors])
    ctrl_flat = ctrl_factor.reshape(ADI * K, -1)
    obsv_flat = obsv_factor.reshape(ADI * K, -1)
    cross_sum = lax.dot_general(ctrl_flat, obsv_flat, (((1,), (1,)), ((), ())), precision=lax.Precision.HIGHEST, preferred_element_type=jnp.float32)
    cross_gram = cross_sum * (1.0 / math.sqrt(NCELLS))
    return (ctrl_factor, obsv_factor, cross_gram)
```

```python
import functools
import math

import jax
import jax.numpy as jnp
from jax import lax
from jax.experimental import pallas as pl
from jax.experimental.pallas import tpu as pltpu
from jax.sharding import PartitionSpec as P

ADI = 2
STEPS = 3
GROUPS = 4
SUB = 8
VMEM_BYTES = 50 * 1024 * 1024


def lookup(region_ids, region_cond):
    summed = jnp.zeros(region_ids.shape, jnp.float32)
    for region in range(region_cond.shape[0]):
        summed = summed + jnp.where(region_ids == region, region_cond[region], jnp.float32(0.0))
    return summed


def solve_polynomial(shift_val, cond_max):
    high_eig = shift_val + 12.0 * cond_max
    mid_eig = 0.5 * (high_eig + shift_val)
    half_span = 0.5 * (high_eig - shift_val)
    ratio_eig = mid_eig / half_span
    rho_now = 1.0 / ratio_eig
    zero = jnp.zeros_like(mid_eig)
    total = [zero] * STEPS
    residual = [jnp.ones_like(mid_eig)] + [zero] * (STEPS - 1)
    direction = [1.0 / mid_eig] + [zero] * (STEPS - 1)
    for step in range(STEPS):
        total = [t + d for t, d in zip(total, direction)]
        if step < STEPS - 1:
            raised = [zero] + direction[:-1]
            residual = [r - (u + shift_val * d) for r, u, d in zip(residual, raised, direction)]
            rho_next = 1.0 / (2.0 * ratio_eig - rho_now)
            direction = [
                rho_next * rho_now * d + 2.0 * rho_next / half_span * r
                for d, r in zip(direction, residual)
            ]
            rho_now = rho_next
    return total


def factor_scalars(shifts, cond_max):
    first = solve_polynomial(shifts[0], cond_max)
    second = solve_polynomial(shifts[1], cond_max)
    scale_first = jnp.sqrt(2.0 * shifts[0])
    scale_second = jnp.sqrt(2.0 * shifts[1]) / scale_first
    both = shifts[0] + shifts[1]
    rest = [1.0 - both * second[0], -both * second[1], -both * second[2]]
    return jnp.stack([scale_first * c for c in first] + [scale_second * c for c in rest])


def face_arrays(cond, valid):
    below = jnp.pad(cond, ((1, 0), (0, 0), (0, 0)))[:-1]
    above = jnp.pad(cond, ((0, 1), (0, 0), (0, 0)))[1:]
    row_next = jnp.pad(cond, ((0, 0), (0, 1), (0, 0)))[:, 1:]
    row_prev = jnp.pad(cond, ((0, 0), (1, 0), (0, 0)))[:, :-1]
    lane_next = jnp.pad(cond, ((0, 0), (0, 0), (0, 1)))[:, :, 1:]
    lane_prev = jnp.pad(cond, ((0, 0), (0, 0), (1, 0)))[:, :, :-1]
    neighbours = above + below + row_next + row_prev + lane_next + lane_prev
    here = valid[:, None, None]
    diag = jnp.where(here, 0.5 * (6.0 * cond + neighbours), 0.0)
    valid_next = jnp.concatenate([valid[1:], jnp.zeros((1,), bool)])[:, None, None]
    row = lax.broadcasted_iota(jnp.int32, cond.shape, 1)
    lane = lax.broadcasted_iota(jnp.int32, cond.shape, 2)
    face_x = jnp.where(here & valid_next, -0.5 * (cond + above), 0.0)
    face_yn = jnp.where(row < cond.shape[1] - 1, -0.5 * (cond + row_next), 0.0)
    face_yp = jnp.where(row > 0, -0.5 * (cond + row_prev), 0.0)
    face_zn = jnp.where(lane < cond.shape[2] - 1, -0.5 * (cond + lane_next), 0.0)
    face_zp = jnp.where(lane > 0, -0.5 * (cond + lane_prev), 0.0)
    return (diag, face_x, face_yn, face_yp, face_zn, face_zp)


def factor_kernel(parts, scal, side, lo, mid, hi, dg, fx, fyn, fyp, fzn, fzp, keep, send, b, y, z):
    cols, per = mid.shape[1], mid.shape[2]
    rows, lanes = mid.shape[3], mid.shape[4]
    own = 2 * per
    window = 3 * own
    part_rows = rows // parts
    steps = rows // SUB
    parity = side[0]

    def gather(i, carry):
        r = pl.multiple_of(i * SUB, SUB)
        for block, source in enumerate((lo, mid, hi)):
            for half in range(2):
                spot = parity if half == 0 else 1 - parity
                start = (block * own + spot * per) * rows
                for layer in range(per):
                    to = pl.multiple_of(start + layer * rows + r, SUB)
                    for c in range(cols):
                        b[c, pl.ds(to, SUB), :] = source[half, c, layer, pl.ds(r, SUB), :]
        return carry

    lax.fori_loop(0, steps, gather, 0)

    def sweep(ref, first, count, r, emit):
        def at(layer, shift=0):
            spot = layer * rows + r
            return pl.ds(spot + shift if shift else pl.multiple_of(spot, SUB), SUB)

        below = [ref[c, at(first - 1), :] for c in range(cols)]
        here = [ref[c, at(first), :] for c in range(cols)]
        face_low = fx[at(first - 1), :]
        for step in range(count):
            layer = first + step
            above = [ref[c, at(layer + 1), :] for c in range(cols)]
            face_high = fx[at(layer), :]
            diag = dg[at(layer), :]
            row_n, row_p = fyn[at(layer), :], fyp[at(layer), :]
            lane_n, lane_p = fzn[at(layer), :], fzp[at(layer), :]
            for c in range(cols):
                v = here[c]
                applied = diag * v + face_high * above[c] + face_low * below[c]
                applied += row_n * ref[c, at(layer, 1), :] + row_p * ref[c, at(layer, -1), :]
                applied += lane_n * pltpu.roll(v, lanes - 1, 1) + lane_p * pltpu.roll(v, 1, 1)
                emit(layer, c, v, applied)
            below, here, face_low = here, above, face_high

    def store(ref, layer, c, r, value):
        ref[c, pl.ds(pl.multiple_of(layer * rows + r, SUB), SUB), :] = value

    def load(ref, layer, c, r):
        return ref[c, pl.ds(pl.multiple_of(layer * rows + r, SUB), SUB), :]

    def first_half(i, carry):
        r = i * SUB
        sweep(b, 1, window - 2, r, lambda l, c, v, a: store(y, l, c, r, scal[1] * v + scal[2] * a))
        return carry

    def first_end(i, carry):
        r = i * SUB
        sweep(y, 2, window - 4, r, lambda l, c, v, a: store(z, l, c, r, scal[0] * load(b, l, c, r) + a))
        return carry

    def second_half(i, carry):
        r = i * SUB
        sweep(z, 3, window - 6, r, lambda l, c, v, a: store(y, l, c, r, scal[4] * v + scal[5] * a))
        return carry

    def second_end(i, carry):
        r = i * SUB
        part = i // (part_rows // SUB)
        inner = pl.ds(pl.multiple_of((i - part * (part_rows // SUB)) * SUB, SUB), SUB)
        for out, spot in ((keep, parity), (send, 1 - parity)):
            base = own + spot * per

            def emit(l, c, v, a):
                w = load(z, l, c, r)
                out[part, 0, c, l - base, inner, :] = w
                out[part, 1, c, l - base, inner, :] = scal[3] * w + a

            for layer in range(per):

                def emit_one(l, c, v, a, layer=layer):
                    w = load(z, l, c, r)
                    out[part, 0, c, layer, inner, :] = w
                    out[part, 1, c, layer, inner, :] = scal[3] * w + a

                sweep(y, base + layer, 1, r, emit_one)
        return carry

    for stage in (first_half, first_end, second_half, second_end):
        lax.fori_loop(0, steps, stage, 0)


def factors(parts, cols, scal, side, lo, mid, hi, faces):
    _, total, per, rows, lanes = mid.shape
    layers = 6 * per
    block = pl.BlockSpec((2, cols, per, rows, lanes), lambda i: (0, i, 0, 0, 0))
    out_block = pl.BlockSpec((parts, ADI, cols, per, rows // parts, lanes), lambda i: (0, 0, i, 0, 0, 0))
    out_shape = jax.ShapeDtypeStruct((parts, ADI, total, per, rows // parts, lanes), jnp.float32)
    work = total * layers * rows * lanes
    return pl.pallas_call(
        functools.partial(factor_kernel, parts),
        grid=(total // cols,),
        out_shape=(out_shape, out_shape),
        in_specs=[pl.BlockSpec(memory_space=pltpu.SMEM)] * 2
        + [block] * 3
        + [pl.BlockSpec(memory_space=pltpu.VMEM)] * 6,
        out_specs=(out_block, out_block),
        scratch_shapes=[pltpu.VMEM((cols, layers * rows, lanes), jnp.float32)] * 3,
        compiler_params=pltpu.CompilerParams(vmem_limit_bytes=VMEM_BYTES),
        cost_estimate=pl.CostEstimate(flops=40 * work, bytes_accessed=8 * work, transcendentals=0),
        name="factors",
    )(scal, side, lo, mid, hi, *faces)


def place_kernel(side, keep, recv, *refs):
    ctrl, obsv = refs[-2:]
    half = keep.shape[2] // 2
    parity = side[0]
    for source, spot in ((keep, parity), (recv, 1 - parity)):
        for adi in range(ADI):
            ctrl[adi, 0, spot, 0] = source[0, adi, :half]
            obsv[adi, 0, spot, 0] = source[0, adi, half:]


def place(group, groups, side, keep, recv, held):
    parts, adi, cols, per, rows, lanes = keep.shape
    half = cols // 2
    block = pl.BlockSpec((1, adi, cols, per, rows, lanes), lambda i: (i, 0, 0, 0, 0, 0))
    out_block = pl.BlockSpec(
        (adi, 1, 2, 1, half, per, rows, lanes), lambda i: (0, i, 0, group, 0, 0, 0, 0)
    )
    out_shape = jax.ShapeDtypeStruct((adi, parts, 2, groups, half, per, rows, lanes), jnp.float32)
    size = 4 * keep.size
    return pl.pallas_call(
        place_kernel,
        grid=(parts,),
        out_shape=(out_shape, out_shape),
        in_specs=[pl.BlockSpec(memory_space=pltpu.SMEM), block, block]
        + [pl.BlockSpec(memory_space=pl.ANY)] * len(held),
        out_specs=(out_block, out_block),
        input_output_aliases={3 + i: i for i in range(len(held))},
        compiler_params=pltpu.CompilerParams(vmem_limit_bytes=VMEM_BYTES),
        cost_estimate=pl.CostEstimate(flops=0, bytes_accessed=4 * size, transcendentals=0),
        name="place",
    )(side, keep, recv, *held)


def split16(value):
    high = value.astype(jnp.bfloat16)
    return high, (value - high.astype(jnp.float32)).astype(jnp.bfloat16)


def gram_kernel(ctrl, obsv, out, left, right):
    adi, cols, _, rows, lanes = ctrl.shape
    total = adi * cols

    @pl.when((pl.program_id(0) == 0) & (pl.program_id(1) == 0))
    def _():
        out[...] = jnp.zeros_like(out)

    for a in range(adi):
        left[pl.ds(a * cols * rows, cols * rows), :] = ctrl[a, :, 0].reshape(cols * rows, lanes)
        right[pl.ds(a * cols * rows, cols * rows), :] = obsv[a, :, 0].reshape(cols * rows, lanes)

    def pair(ref, row):
        values = [ref[pl.ds(row + k, total, stride=rows), :] for k in range(2)]
        return split16(jnp.concatenate(values, axis=1))

    def dot(a, b):
        return lax.dot_general(a, b, (((1,), (1,)), ((), ())), preferred_element_type=jnp.float32)

    summed = out[...]
    for row in range(0, rows, 2):
        a_high, a_low = pair(left, row)
        b_high, b_low = pair(right, row)
        summed = summed + (dot(a_high, b_high) + (dot(a_high, b_low) + dot(a_low, b_high)))
    out[...] = summed


def gram(ctrl, obsv):
    adi, cols, per, rows, lanes = ctrl.shape
    chunk = 16
    block = pl.BlockSpec((adi, cols, 1, chunk, lanes), lambda i, j: (0, 0, i, j, 0))
    total = adi * cols
    return pl.pallas_call(
        gram_kernel,
        grid=(per, rows // chunk),
        out_shape=jax.ShapeDtypeStruct((total, total), jnp.float32),
        in_specs=[block, block],
        out_specs=pl.BlockSpec((total, total), lambda i, j: (0, 0)),
        scratch_shapes=[pltpu.VMEM((total * chunk, lanes), jnp.float32)] * 2,
        compiler_params=pltpu.CompilerParams(vmem_limit_bytes=VMEM_BYTES),
        cost_estimate=pl.CostEstimate(
            flops=6 * total * total * per * rows * lanes, bytes_accessed=8 * ctrl.size, transcendentals=0
        ),
        name="gram",
    )(ctrl, obsv)


def body(input_map, output_map, region_ids, region_cond, shift_ids):
    slabs, parts = lax.axis_size("slab"), lax.axis_size("col")
    col_local, per, rows, lanes = input_map.shape
    total_x = per * slabs
    slab = lax.axis_index("slab")
    parity = lax.rem(slab, 2)
    side = parity.reshape(1).astype(jnp.int32)
    swap = [(i, i ^ 1) for i in range(slabs)]
    upward = [(i, i + 2) for i in range(slabs - 2)]
    downward = [(i + 2, i) for i in range(slabs - 2)]

    cond_max = jnp.max(region_cond)
    shifts = 0.25 * jnp.exp2(shift_ids.astype(jnp.float32))
    scal = factor_scalars(shifts, cond_max)

    half = col_local // 2
    width = half // GROUPS

    def columns(spot, group):
        start = spot * half + group * width
        return [lax.dynamic_slice_in_dim(m, start, width, 0) for m in (input_map, output_map)]

    swapped = []
    after = None
    for group in range(GROUPS):
        outgoing = jnp.concatenate(columns(1 - parity, group), 0)
        if after is not None:
            outgoing, after = lax.optimization_barrier((outgoing, after))
        after = lax.ppermute(outgoing, "slab", swap)
        swapped.append(after)
        if group == 0:
            cond_own = lookup(region_ids, region_cond)
            cond_other = lax.ppermute(cond_own, "slab", swap)
            even = parity == 0
            cond_pair = jnp.concatenate(
                [jnp.where(even, cond_own, cond_other), jnp.where(even, cond_other, cond_own)], 0
            )
            cond = jnp.concatenate(
                [
                    lax.ppermute(cond_pair, "slab", upward),
                    cond_pair,
                    lax.ppermute(cond_pair, "slab", downward),
                ],
                0,
            )
            layer = (slab // 2 - 1) * 2 * per + jnp.arange(6 * per)
            faces = [
                f.reshape(6 * per * rows, lanes)
                for f in face_arrays(cond, (layer >= 0) & (layer < total_x))
            ]

    held = ()
    after = None
    for group in range(GROUPS):
        mid = jnp.stack([jnp.concatenate(columns(parity, group), 0), swapped[group]])
        if after is not None:
            mid, after = lax.optimization_barrier((mid, after))
        lo = lax.ppermute(mid, "slab", upward)
        hi = lax.ppermute(mid, "slab", downward)
        after = (lo, hi)
        keep, send = factors(parts, 2, scal, side, lo, mid, hi, faces)
        recv = lax.ppermute(send, "slab", swap)
        keep, recv = (
            lax.all_to_all(x, "col", split_axis=0, concat_axis=0, tiled=True) for x in (keep, recv)
        )
        held = place(group, GROUPS, side, keep, recv, held)

    ctrl, obsv = (x.reshape(ADI, parts * col_local, per, rows // parts, lanes) for x in held)
    partial_value = gram(ctrl, obsv)
    count = partial_value.shape[0]
    tiles = partial_value.reshape(slabs, count // slabs, parts, count // parts).transpose(0, 2, 1, 3)
    tiles = tiles.reshape(slabs * parts, count // slabs, count // parts)
    tiles = lax.all_to_all(tiles, ("slab", "col"), split_axis=0, concat_axis=0, tiled=True)
    norm_scale = 1.0 / math.sqrt(total_x * rows * lanes)
    return (ctrl, obsv, jnp.sum(tiles, 0) * norm_scale)


def solution(mesh):
    placed = (
        P("col", "slab", None, None),
        P("col", "slab", None, None),
        P("slab", None, None),
        P(),
        P(),
    )
    return jax.shard_map(
        body,
        mesh=mesh,
        in_specs=placed,
        out_specs=(
            P(None, None, "slab", "col", None),
            P(None, None, "slab", "col", None),
            P("slab", "col"),
        ),
        check_vma=False,
    )
```

```python
import functools
import math

import jax
import jax.numpy as jnp
from jax import lax
from jax.experimental import pallas as pl
from jax.experimental.pallas import tpu as pltpu
from jax.sharding import PartitionSpec as P

ADI = 2
STEPS = 3
GROUPS = 4
SUB = 8
VMEM_BYTES = 50 * 1024 * 1024
ANY = pl.BlockSpec(memory_space=pl.ANY)
SCALARS = pl.BlockSpec(memory_space=pltpu.SMEM)


def solve_polynomial(shift_val, cond_max):
    high_eig = shift_val + 12.0 * cond_max
    mid_eig = 0.5 * (high_eig + shift_val)
    half_span = 0.5 * (high_eig - shift_val)
    ratio_eig = mid_eig / half_span
    rho_now = 1.0 / ratio_eig
    zero = jnp.zeros_like(mid_eig)
    total = [zero] * STEPS
    residual = [jnp.ones_like(mid_eig)] + [zero] * (STEPS - 1)
    direction = [1.0 / mid_eig] + [zero] * (STEPS - 1)
    for step in range(STEPS):
        total = [t + d for t, d in zip(total, direction)]
        if step < STEPS - 1:
            raised = [zero] + direction[:-1]
            residual = [r - (u + shift_val * d) for r, u, d in zip(residual, raised, direction)]
            rho_next = 1.0 / (2.0 * ratio_eig - rho_now)
            direction = [
                rho_next * rho_now * d + 2.0 * rho_next / half_span * r
                for d, r in zip(direction, residual)
            ]
            rho_now = rho_next
    return total


def factor_scalars(shifts, cond_max):
    first = solve_polynomial(shifts[0], cond_max)
    second = solve_polynomial(shifts[1], cond_max)
    scale_first = jnp.sqrt(2.0 * shifts[0])
    scale_second = jnp.sqrt(2.0 * shifts[1]) / scale_first
    both = shifts[0] + shifts[1]
    rest = [1.0 - both * second[0], -both * second[1], -both * second[2]]
    return jnp.stack([scale_first * c for c in first] + [scale_second * c for c in rest])


def pack(side, sources, pieces, counts, after=(), ids=None):
    size, lanes = sources[0].shape[1:]
    held = len(sources) + len(after) + (ids is not None)

    def kernel(*refs):
        side_ref, operands = refs[0], refs[1 : 1 + held]
        outs = refs[1 + held : 1 + held + len(counts)]
        rest = refs[1 + held + len(counts) :]
        sems = rest[-1]
        copies = []
        order = sorted(range(len(pieces)), key=lambda k: pieces[k][0] is None)
        filled = False
        for k in order:
            source, start, step, count, out, to = pieces[k]
            if source is None:
                if not filled:
                    rest[0][0] = (operands[held - 1][...] + 1).astype(jnp.float32)
                    filled = True
                block = rest[0]
            else:
                block = operands[source].at[pl.ds(start + step * side_ref[0], count)]
            copy = pltpu.make_async_copy(block, outs[out].at[pl.ds(to, count)], sems.at[k])
            copy.start()
            copies.append(copy)
        for copy in copies:
            copy.wait()

    scratch = [pltpu.SemaphoreType.DMA((len(pieces),))]
    extra, specs = [], []
    if ids is not None:
        scratch = [pltpu.VMEM((1, size, lanes), jnp.float32)] + scratch
        extra, specs = [ids], [pl.BlockSpec(memory_space=pltpu.VMEM)]
    moved = 4 * sum(p[3] for p in pieces) * size * lanes
    return pl.pallas_call(
        kernel,
        out_shape=[jax.ShapeDtypeStruct((c, size, lanes), jnp.float32) for c in counts],
        in_specs=[SCALARS] + [ANY] * (len(sources) + len(after)) + specs,
        out_specs=[ANY] * len(counts),
        scratch_shapes=scratch,
        compiler_params=pltpu.CompilerParams(vmem_limit_bytes=VMEM_BYTES),
        cost_estimate=pl.CostEstimate(flops=0, bytes_accessed=2 * moved, transcendentals=0),
        name="pack",
    )(side, *sources, *after, *extra)


def factor_kernel(spots, parts, rows, side, scal, table, *refs):
    data, (out, b, y, z, cond, dg, fx, fyn, fyp, fzn, fzp, sems) = refs[: len(spots)], refs[len(spots) :]
    cols, size, lanes = b.shape
    window = size // rows
    per = window // 6
    own = 2 * per
    slab = per * rows
    part_rows = rows // parts
    steps = rows // SUB
    parity = side[0]

    copies = []
    for k, (start, count, block, other, to) in enumerate(spots):
        spot = 1 - parity if other else parity
        at = pl.ds(pl.multiple_of((block * 2 + spot) * slab, SUB), slab)
        if count == 0:
            copy = pltpu.make_async_copy(data[k].at[start], fx.at[at], sems.at[k])
        else:
            place_at = b.at[pl.ds(to, count), at]
            if isinstance(start, tuple):
                start = start[0] + start[1] * parity
            copy = pltpu.make_async_copy(data[k].at[pl.ds(start, count)], place_at, sems.at[k])
        copy.start()
        copies.append(copy)

    def wait(ids):
        for (_, count, *_), copy in zip(spots, copies):
            if (count == 0) == ids:
                copy.wait()

    def at(layer, r, shift=0):
        spot = layer * rows + r
        return pl.ds(spot + shift if shift else pl.multiple_of(spot, SUB), SUB)

    wait(True)
    levels = [table[k] for k in range(table.shape[0])]

    def fill(i, carry):
        r = i * SUB
        for layer in range(window):
            index = fx[at(layer, r), :]
            value = jnp.zeros_like(index)
            for k, level in enumerate(levels):
                value = jnp.where(index == float(k + 1), level, value)
            cond[at(layer, r), :] = value
        return carry

    lax.fori_loop(0, steps, fill, 0)
    row = lax.broadcasted_iota(jnp.int32, (SUB, lanes), 0)
    lane = lax.broadcasted_iota(jnp.int32, (SUB, lanes), 1)

    def prepare(i, carry):
        r = i * SUB
        below, here = cond[at(0, r), :], cond[at(1, r), :]
        fx[at(0, r), :] = jnp.where((below > 0) & (here > 0), -0.5 * (below + here), 0.0)
        for layer in range(1, window - 1):
            above = cond[at(layer + 1, r), :]
            row_n = jnp.where(row + r < rows - 1, cond[at(layer, r, 1), :], 0.0)
            row_p = jnp.where(row + r > 0, cond[at(layer, r, -1), :], 0.0)
            lane_n = jnp.where(lane < lanes - 1, pltpu.roll(here, lanes - 1, 1), 0.0)
            lane_p = jnp.where(lane > 0, pltpu.roll(here, 1, 1), 0.0)
            around = (above + below) + (row_n + row_p) + (lane_n + lane_p)
            dg[at(layer, r), :] = jnp.where(here > 0, 0.5 * (6.0 * here + around), 0.0)

            def face(other):
                return jnp.where((here > 0) & (other > 0), -0.5 * (here + other), 0.0)

            fx[at(layer, r), :] = face(above)
            fyn[at(layer, r), :] = face(row_n)
            fyp[at(layer, r), :] = face(row_p)
            fzn[at(layer, r), :] = face(lane_n)
            fzp[at(layer, r), :] = face(lane_p)
            below, here = here, above
        return carry

    lax.fori_loop(0, steps, prepare, 0)
    full = [jnp.full((SUB, lanes), scal[k], jnp.float32) for k in range(6)]
    wait(False)

    def sweep(ref, first, count, r, emit):
        below = [ref[c, at(first - 1, r), :] for c in range(cols)]
        here = [ref[c, at(first, r), :] for c in range(cols)]
        face_low = fx[at(first - 1, r), :]
        for layer in range(first, first + count):
            above = [ref[c, at(layer + 1, r), :] for c in range(cols)]
            face_high = fx[at(layer, r), :]
            diag = dg[at(layer, r), :]
            row_n, row_p = fyn[at(layer, r), :], fyp[at(layer, r), :]
            lane_n, lane_p = fzn[at(layer, r), :], fzp[at(layer, r), :]
            for c in range(cols):
                v = here[c]
                along_x = face_high * above[c] + face_low * below[c]
                along_y = row_n * ref[c, at(layer, r, 1), :] + row_p * ref[c, at(layer, r, -1), :]
                along_z = lane_n * pltpu.roll(v, lanes - 1, 1) + lane_p * pltpu.roll(v, 1, 1)
                emit(layer, c, v, (diag * v + along_x) + (along_y + along_z))
            below, here, face_low = here, above, face_high

    def store(ref, layer, c, r, value):
        ref[c, at(layer, r), :] = value

    def first_half(i, carry):
        r = i * SUB
        sweep(b, 1, window - 2, r, lambda l, c, v, a: store(y, l, c, r, full[1] * v + full[2] * a))
        return carry

    def first_end(i, carry):
        r = i * SUB
        sweep(y, 2, window - 4, r, lambda l, c, v, a: store(z, l, c, r, full[0] * b[c, at(l, r), :] + a))
        return carry

    def second_half(i, carry):
        r = i * SUB
        sweep(z, 3, window - 6, r, lambda l, c, v, a: store(y, l, c, r, full[4] * v + full[5] * a))
        return carry

    def second_end(i, carry):
        r = i * SUB
        sweep(y, own, own, r, lambda l, c, v, a: store(b, l, c, r, full[3] * z[c, at(l, r), :] + a))
        return carry

    base = len(spots)
    leaving = []

    def leave(ref, adi, part):
        for layer in range(own):
            spot = (own + layer) * rows + part * part_rows
            copy = pltpu.make_async_copy(
                ref.at[:, pl.ds(spot, part_rows)],
                out.at[layer // per, part, adi, :, layer % per],
                sems.at[base + len(leaving)],
            )
            copy.start()
            leaving.append(copy)

    lax.fori_loop(0, steps, first_half, 0)
    lax.fori_loop(0, steps, first_end, 0)
    for part in range(parts):
        leave(z, 0, part)
    lax.fori_loop(0, steps, second_half, 0)
    for part in range(parts):
        lax.fori_loop(part * steps // parts, (part + 1) * steps // parts, second_end, 0)
        leave(b, 1, part)
    for copy in leaving:
        copy.wait()


def factors(parts, cols, rows, per, side, scal, table, pieces):
    lanes = pieces[0][0].shape[-1]
    layers = 6 * per
    size = layers * rows
    work = cols * size * lanes
    out = (2, parts, ADI, cols, per, rows // parts, lanes)
    spots = [p[1:] for p in pieces]
    flat = pltpu.VMEM((size, lanes), jnp.float32)
    return pl.pallas_call(
        functools.partial(factor_kernel, spots, parts, rows),
        out_shape=jax.ShapeDtypeStruct(out, jnp.float32),
        in_specs=[SCALARS] * 3 + [ANY] * len(pieces),
        out_specs=ANY,
        scratch_shapes=[pltpu.VMEM((cols, size, lanes), jnp.float32)] * 3
        + [flat] * 7
        + [pltpu.SemaphoreType.DMA((len(pieces) + 2 * ADI * per * parts,))],
        compiler_params=pltpu.CompilerParams(vmem_limit_bytes=VMEM_BYTES),
        cost_estimate=pl.CostEstimate(flops=40 * work, bytes_accessed=8 * work, transcendentals=0),
        name="factors",
    )(side, scal, table, *(p[0] for p in pieces))


def place_kernel(moved, *refs):
    ctrl, obsv = refs[-2:]
    half = moved.shape[3] // 2
    for spot in range(2):
        for adi in range(ADI):
            ctrl[adi, 0, spot, 0] = moved[spot, 0, adi, :half]
            obsv[adi, 0, spot, 0] = moved[spot, 0, adi, half:]


def place(group, groups, moved, held):
    _, parts, adi, cols, per, rows, lanes = moved.shape
    half = cols // 2
    block = pl.BlockSpec((2, 1, adi, cols, per, rows, lanes), lambda i: (0, i, 0, 0, 0, 0, 0))
    out_block = pl.BlockSpec(
        (adi, 1, 2, 1, half, per, rows, lanes), lambda i: (0, i, 0, group, 0, 0, 0, 0)
    )
    out_shape = jax.ShapeDtypeStruct((adi, parts, 2, groups, half, per, rows, lanes), jnp.float32)
    return pl.pallas_call(
        place_kernel,
        grid=(parts,),
        out_shape=(out_shape, out_shape),
        in_specs=[block] + [ANY] * len(held),
        out_specs=(out_block, out_block),
        input_output_aliases={1 + i: i for i in range(len(held))},
        compiler_params=pltpu.CompilerParams(vmem_limit_bytes=VMEM_BYTES),
        cost_estimate=pl.CostEstimate(flops=0, bytes_accessed=8 * moved.size, transcendentals=0),
        name="place",
    )(moved, *held)


def split16(value):
    high = value.astype(jnp.bfloat16)
    return high, (value - high.astype(jnp.float32)).astype(jnp.bfloat16)


def gram_kernel(ctrl, obsv, out, left, right):
    adi, cols, _, rows, lanes = ctrl.shape
    total = adi * cols

    @pl.when((pl.program_id(0) == 0) & (pl.program_id(1) == 0))
    def _():
        out[...] = jnp.zeros_like(out)

    for a in range(adi):
        left[pl.ds(a * cols * rows, cols * rows), :] = ctrl[a, :, 0].reshape(cols * rows, lanes)
        right[pl.ds(a * cols * rows, cols * rows), :] = obsv[a, :, 0].reshape(cols * rows, lanes)

    def pair(ref, row):
        values = [ref[pl.ds(row + k, total, stride=rows), :] for k in range(2)]
        return split16(jnp.concatenate(values, axis=1))

    def dot(a, b):
        return lax.dot_general(a, b, (((1,), (1,)), ((), ())), preferred_element_type=jnp.float32)

    summed = out[...]
    for row in range(0, rows, 2):
        a_high, a_low = pair(left, row)
        b_high, b_low = pair(right, row)
        summed = summed + (dot(a_high, b_high) + (dot(a_high, b_low) + dot(a_low, b_high)))
    out[...] = summed


def gram(ctrl, obsv):
    adi, cols, per, rows, lanes = ctrl.shape
    chunk = 16
    block = pl.BlockSpec((adi, cols, 1, chunk, lanes), lambda i, j: (0, 0, i, j, 0))
    total = adi * cols
    return pl.pallas_call(
        gram_kernel,
        grid=(per, rows // chunk),
        out_shape=jax.ShapeDtypeStruct((total, total), jnp.float32),
        in_specs=[block, block],
        out_specs=pl.BlockSpec((total, total), lambda i, j: (0, 0)),
        scratch_shapes=[pltpu.VMEM((total * chunk, lanes), jnp.float32)] * 2,
        compiler_params=pltpu.CompilerParams(vmem_limit_bytes=VMEM_BYTES),
        cost_estimate=pl.CostEstimate(
            flops=6 * total * total * per * rows * lanes, bytes_accessed=8 * ctrl.size, transcendentals=0
        ),
        name="gram",
    )(ctrl, obsv)


def body(input_map, output_map, region_ids, region_cond, shift_ids):
    slabs, parts = lax.axis_size("slab"), lax.axis_size("col")
    col_local, per, rows, lanes = input_map.shape
    total_x = per * slabs
    parity = lax.rem(lax.axis_index("slab"), 2)
    side = parity.reshape(1).astype(jnp.int32)
    swap = [(i, i ^ 1) for i in range(slabs)]
    upward = [(i, i + 2) for i in range(slabs - 2)]
    downward = [(i + 2, i) for i in range(slabs - 2)]

    cond_max = jnp.max(region_cond)
    shifts = 0.25 * jnp.exp2(shift_ids.astype(jnp.float32))
    scal = factor_scalars(shifts, cond_max)

    maps = [m.reshape(col_local, per * rows, lanes) for m in (input_map, output_map)]
    ids = region_ids.reshape(per * rows, lanes)
    half = col_local // 2
    width = half // GROUPS
    n = 2 * width

    def exchange(x):
        return lax.ppermute(x, "slab", swap)

    def halo(x):
        return lax.ppermute(x, "slab", upward), lax.ppermute(x, "slab", downward)

    def kept(group, out, to, first=0):
        return [(first + k, group * width, half, width, out, to + k * width) for k in range(2)]

    def sent(group, out, to, first=0, groups=1):
        return [
            (first + k, half + group * width, -half, groups * width, out, to + k * groups * width)
            for k in range(2)
        ]

    pieces = sent(0, 0, 0) + [(None, 0, 0, 1, 0, n)] + kept(0, 1, 0) + [(None, 0, 0, 1, 1, n)]
    outgoing, message = pack(side, maps, pieces, (n + 1, n + 1), ids=ids)
    got = [(exchange(outgoing), 0)]
    halos = [halo(message)]

    pieces = (
        [(0, 0, 0, n, 0, 0), (0, n, 0, 1, 0, 2 * n)] + kept(1, 0, n, 1) + sent(1, 1, 0, 1)
    )
    message, outgoing = pack(side, [got[0][0]] + maps, pieces, (2 * n + 1, n))
    got.append((exchange(outgoing), 0))
    halos.append(halo(message))

    outgoing, next_outgoing = pack(
        side, maps, sent(2, 0, 0) + sent(3, 1, 0), (n, n), after=(got[1][0],)
    )
    got.append((exchange(outgoing), 0))
    next_outgoing, _ = lax.optimization_barrier((next_outgoing, got[2][0]))
    got.append((exchange(next_outgoing), 0))

    region_float = (ids + 1).astype(jnp.float32)[None]
    held = ()
    for group in range(GROUPS):
        if group + 2 <= GROUPS:
            source = got[group + 1][0]
            pieces = [(0, 0, 0, n, 0, 0)]
            if group + 2 < GROUPS:
                pieces += kept(group + 2, 0, n, 1)
            count = sum(p[3] for p in pieces)
            (message,) = pack(side, [source] + maps, pieces, (count,), after=halos[-1])
            halos.append(halo(message))
        (lo_kept, hi_kept), (lo_got, hi_got) = halos[group], halos[group + 1]
        start = 0 if group == 0 else n
        (lo_a, hi_a), (lo_b, hi_b) = halos[0], halos[1]
        pieces = [
            (lo_a, n, 0, 0, False, 0),
            (hi_a, n, 0, 2, False, 0),
            (lo_b, 2 * n, 0, 0, True, 0),
            (hi_b, 2 * n, 0, 2, True, 0),
            (region_float, 0, 0, 1, False, 0),
            (got[0][0], n, 0, 1, True, 0),
            (lo_kept, start, n, 0, False, 0),
            (hi_kept, start, n, 2, False, 0),
            (maps[0], (group * width, half), width, 1, False, 0),
            (maps[1], (group * width, half), width, 1, False, width),
            (got[group][0], 0, n, 1, True, 0),
            (lo_got, 0, n, 0, True, 0),
            (hi_got, 0, n, 2, True, 0),
        ]
        result = factors(parts, n, rows, per, side, scal, region_cond, pieces)
        result = result.reshape(2 * parts, *result.shape[2:])
        pairs = [[k * 2 * parts + j for j in range(2 * parts)] for k in range(slabs // 2)]
        moved = lax.all_to_all(
            result, ("slab", "col"), split_axis=0, concat_axis=0, axis_index_groups=pairs, tiled=True
        )
        held = place(group, GROUPS, moved.reshape(2, parts, *moved.shape[1:]), held)

    ctrl, obsv = (x.reshape(ADI, parts * col_local, per, rows // parts, lanes) for x in held)
    partial_value = gram(ctrl, obsv)
    count = partial_value.shape[0]
    tiles = partial_value.reshape(slabs, count // slabs, parts, count // parts).transpose(0, 2, 1, 3)
    tiles = tiles.reshape(slabs * parts, count // slabs, count // parts)
    tiles = lax.all_to_all(tiles, ("slab", "col"), split_axis=0, concat_axis=0, tiled=True)
    norm_scale = 1.0 / math.sqrt(total_x * rows * lanes)
    return (ctrl, obsv, jnp.sum(tiles, 0) * norm_scale)


def solution(mesh):
    placed = (
        P("col", "slab", None, None),
        P("col", "slab", None, None),
        P("slab", None, None),
        P(),
        P(),
    )
    return jax.shard_map(
        body,
        mesh=mesh,
        in_specs=placed,
        out_specs=(
            P(None, None, "slab", "col", None),
            P(None, None, "slab", "col", None),
            P("slab", "col"),
        ),
        check_vma=False,
    )
```

```python
import functools
import math

import jax
import jax.numpy as jnp
from jax import lax
from jax.experimental import pallas as pl
from jax.experimental.pallas import tpu as pltpu
from jax.sharding import PartitionSpec as P

ADI = 2
STEPS = 3
GROUPS = 4
SUB = 8
VMEM_BYTES = 50 * 1024 * 1024
ANY = pl.BlockSpec(memory_space=pl.ANY)
IN_VMEM = pl.BlockSpec(memory_space=pltpu.VMEM)
SCALARS = pl.BlockSpec(memory_space=pltpu.SMEM)


def solve_polynomial(shift_val, cond_max):
    high_eig = shift_val + 12.0 * cond_max
    mid_eig = 0.5 * (high_eig + shift_val)
    half_span = 0.5 * (high_eig - shift_val)
    ratio_eig = mid_eig / half_span
    rho_now = 1.0 / ratio_eig
    zero = jnp.zeros_like(mid_eig)
    total = [zero] * STEPS
    residual = [jnp.ones_like(mid_eig)] + [zero] * (STEPS - 1)
    direction = [1.0 / mid_eig] + [zero] * (STEPS - 1)
    for step in range(STEPS):
        total = [t + d for t, d in zip(total, direction)]
        if step < STEPS - 1:
            raised = [zero] + direction[:-1]
            residual = [r - (u + shift_val * d) for r, u, d in zip(residual, raised, direction)]
            rho_next = 1.0 / (2.0 * ratio_eig - rho_now)
            direction = [
                rho_next * rho_now * d + 2.0 * rho_next / half_span * r
                for d, r in zip(direction, residual)
            ]
            rho_now = rho_next
    return total


def factor_scalars(shifts, cond_max):
    first = solve_polynomial(shifts[0], cond_max)
    second = solve_polynomial(shifts[1], cond_max)
    scale_first = jnp.sqrt(2.0 * shifts[0])
    scale_second = jnp.sqrt(2.0 * shifts[1]) / scale_first
    both = shifts[0] + shifts[1]
    rest = [1.0 - both * second[0], -both * second[1], -both * second[2]]
    return jnp.stack([scale_first * c for c in first] + [scale_second * c for c in rest])


def pack(side, sources, pieces, counts, after=(), ids=None):
    size, lanes = sources[0].shape[1:]
    held = len(sources) + len(after) + (ids is not None)

    def kernel(*refs):
        side_ref, operands = refs[0], refs[1 : 1 + held]
        outs = refs[1 + held : 1 + held + len(counts)]
        sems = refs[-1]
        copies = []
        for k, (source, start, step, count, out, to) in enumerate(pieces):
            if source is not None:
                block = operands[source].at[pl.ds(start + step * side_ref[0], count)]
                copy = pltpu.make_async_copy(block, outs[out].at[pl.ds(to, count)], sems.at[k])
                copy.start()
                copies.append(copy)
        for source, _, _, _, out, to in pieces:
            if source is None:
                outs[out][to] = (operands[held - 1][...] + 1).astype(jnp.float32)
        for copy in copies:
            copy.wait()

    extra, specs = ([ids], [IN_VMEM]) if ids is not None else ([], [])
    moved = 4 * sum(p[3] for p in pieces) * size * lanes
    return pl.pallas_call(
        kernel,
        out_shape=[jax.ShapeDtypeStruct((c, size, lanes), jnp.float32) for c in counts],
        in_specs=[SCALARS] + [ANY] * (len(sources) + len(after)) + specs,
        out_specs=[IN_VMEM] * len(counts),
        scratch_shapes=[pltpu.SemaphoreType.DMA((len(pieces),))],
        compiler_params=pltpu.CompilerParams(vmem_limit_bytes=VMEM_BYTES),
        cost_estimate=pl.CostEstimate(flops=0, bytes_accessed=2 * moved, transcendentals=0),
        name="pack",
    )(side, *sources, *after, *extra)


def factor_kernel(spots, parts, rows, side, scal, table, *refs):
    data, (out, b, y, z, cond, dg, fx, fyn, fyp, fzn, fzp, sems) = refs[: len(spots)], refs[-12:]
    cols, size, lanes = b.shape
    window = size // rows
    per = window // 6
    own = 2 * per
    slab = per * rows
    part_rows = rows // parts
    steps = rows // SUB
    parity = side[0]

    copies = []
    for k, (start, count, block, other, to) in enumerate(spots):
        spot = 1 - parity if other else parity
        at = pl.ds(pl.multiple_of((block * 2 + spot) * slab, SUB), slab)
        if count == 0:
            copy = pltpu.make_async_copy(data[k].at[start], fx.at[at], sems.at[k])
        else:
            place_at = b.at[pl.ds(to, count), at]
            if isinstance(start, tuple):
                start = start[0] + start[1] * parity
            copy = pltpu.make_async_copy(data[k].at[pl.ds(start, count)], place_at, sems.at[k])
        copy.start()
        copies.append(copy)

    def wait(ids):
        for (_, count, *_), copy in zip(spots, copies):
            if (count == 0) == ids:
                copy.wait()

    def at(layer, r, shift=0):
        spot = layer * rows + r
        return pl.ds(spot + shift if shift else pl.multiple_of(spot, SUB), SUB)

    wait(True)
    levels = [table[k] for k in range(table.shape[0])]

    def fill(i, carry):
        r = i * SUB
        for layer in range(window):
            index = fx[at(layer, r), :]
            value = jnp.zeros_like(index)
            for k, level in enumerate(levels):
                value = jnp.where(index == float(k + 1), level, value)
            cond[at(layer, r), :] = value
        return carry

    lax.fori_loop(0, steps, fill, 0)
    row = lax.broadcasted_iota(jnp.int32, (SUB, lanes), 0)
    lane = lax.broadcasted_iota(jnp.int32, (SUB, lanes), 1)

    def prepare(i, carry):
        r = i * SUB
        below, here = cond[at(0, r), :], cond[at(1, r), :]
        fx[at(0, r), :] = jnp.where((below > 0) & (here > 0), -0.5 * (below + here), 0.0)
        for layer in range(1, window - 1):
            above = cond[at(layer + 1, r), :]
            row_n = jnp.where(row + r < rows - 1, cond[at(layer, r, 1), :], 0.0)
            row_p = jnp.where(row + r > 0, cond[at(layer, r, -1), :], 0.0)
            lane_n = jnp.where(lane < lanes - 1, pltpu.roll(here, lanes - 1, 1), 0.0)
            lane_p = jnp.where(lane > 0, pltpu.roll(here, 1, 1), 0.0)
            around = (above + below) + (row_n + row_p) + (lane_n + lane_p)
            dg[at(layer, r), :] = jnp.where(here > 0, 0.5 * (6.0 * here + around), 0.0)

            def face(other):
                return jnp.where((here > 0) & (other > 0), -0.5 * (here + other), 0.0)

            fx[at(layer, r), :] = face(above)
            fyn[at(layer, r), :] = face(row_n)
            fyp[at(layer, r), :] = face(row_p)
            fzn[at(layer, r), :] = face(lane_n)
            fzp[at(layer, r), :] = face(lane_p)
            below, here = here, above
        return carry

    lax.fori_loop(0, steps, prepare, 0)
    full = [jnp.full((SUB, lanes), scal[k], jnp.float32) for k in range(6)]
    wait(False)

    def sweep(ref, first, count, r, emit):
        below = [ref[c, at(first - 1, r), :] for c in range(cols)]
        here = [ref[c, at(first, r), :] for c in range(cols)]
        face_low = fx[at(first - 1, r), :]
        for layer in range(first, first + count):
            above = [ref[c, at(layer + 1, r), :] for c in range(cols)]
            face_high = fx[at(layer, r), :]
            diag = dg[at(layer, r), :]
            row_n, row_p = fyn[at(layer, r), :], fyp[at(layer, r), :]
            lane_n, lane_p = fzn[at(layer, r), :], fzp[at(layer, r), :]
            for c in range(cols):
                v = here[c]
                along_x = face_high * above[c] + face_low * below[c]
                along_y = row_n * ref[c, at(layer, r, 1), :] + row_p * ref[c, at(layer, r, -1), :]
                along_z = lane_n * pltpu.roll(v, lanes - 1, 1) + lane_p * pltpu.roll(v, 1, 1)
                emit(layer, c, v, (diag * v + along_x) + (along_y + along_z))
            below, here, face_low = here, above, face_high

    def store(ref, layer, c, r, value):
        ref[c, at(layer, r), :] = value

    def first_half(i, carry):
        r = i * SUB
        sweep(b, 1, window - 2, r, lambda l, c, v, a: store(y, l, c, r, full[1] * v + full[2] * a))
        return carry

    def first_end(i, carry):
        r = i * SUB
        sweep(y, 2, window - 4, r, lambda l, c, v, a: store(z, l, c, r, full[0] * b[c, at(l, r), :] + a))
        return carry

    def second_half(i, carry):
        r = i * SUB
        sweep(z, 3, window - 6, r, lambda l, c, v, a: store(y, l, c, r, full[4] * v + full[5] * a))
        return carry

    def second_end(i, carry):
        r = i * SUB
        sweep(y, own, own, r, lambda l, c, v, a: store(b, l, c, r, full[3] * z[c, at(l, r), :] + a))
        return carry

    base = len(spots)
    leaving = []

    def leave(ref, adi, part):
        for layer in range(own):
            spot = (own + layer) * rows + part * part_rows
            copy = pltpu.make_async_copy(
                ref.at[:, pl.ds(spot, part_rows)],
                out.at[layer // per, part, adi, :, layer % per],
                sems.at[base + len(leaving)],
            )
            copy.start()
            leaving.append(copy)

    lax.fori_loop(0, steps, first_half, 0)
    lax.fori_loop(0, steps, first_end, 0)
    for part in range(parts):
        leave(z, 0, part)
    lax.fori_loop(0, steps, second_half, 0)
    for part in range(parts):
        lax.fori_loop(part * steps // parts, (part + 1) * steps // parts, second_end, 0)
        leave(b, 1, part)
    for copy in leaving:
        copy.wait()


def factors(parts, cols, rows, per, side, scal, table, pieces, after):
    lanes = pieces[0][0].shape[-1]
    layers = 6 * per
    size = layers * rows
    work = cols * size * lanes
    out = (2, parts, ADI, cols, per, rows // parts, lanes)
    spots = [p[1:] for p in pieces]
    flat = pltpu.VMEM((size, lanes), jnp.float32)
    return pl.pallas_call(
        functools.partial(factor_kernel, spots, parts, rows),
        out_shape=jax.ShapeDtypeStruct(out, jnp.float32),
        in_specs=[SCALARS] * 3 + [ANY] * (len(pieces) + len(after)),
        out_specs=ANY,
        scratch_shapes=[pltpu.VMEM((cols, size, lanes), jnp.float32)] * 3
        + [flat] * 7
        + [pltpu.SemaphoreType.DMA((len(pieces) + 2 * ADI * per * parts,))],
        compiler_params=pltpu.CompilerParams(vmem_limit_bytes=VMEM_BYTES),
        cost_estimate=pl.CostEstimate(flops=40 * work, bytes_accessed=8 * work, transcendentals=0),
        name="factors",
    )(side, scal, table, *(p[0] for p in pieces), *after)


def place_kernel(moved, *refs):
    ctrl, obsv = refs[-2:]
    half = moved.shape[3] // 2
    for spot in range(2):
        for adi in range(ADI):
            ctrl[adi, 0, spot, 0] = moved[spot, 0, adi, :half]
            obsv[adi, 0, spot, 0] = moved[spot, 0, adi, half:]


def place(group, groups, moved, held):
    _, parts, adi, cols, per, rows, lanes = moved.shape
    half = cols // 2
    block = pl.BlockSpec((2, 1, adi, cols, per, rows, lanes), lambda i: (0, i, 0, 0, 0, 0, 0))
    out_block = pl.BlockSpec(
        (adi, 1, 2, 1, half, per, rows, lanes), lambda i: (0, i, 0, group, 0, 0, 0, 0)
    )
    out_shape = jax.ShapeDtypeStruct((adi, parts, 2, groups, half, per, rows, lanes), jnp.float32)
    return pl.pallas_call(
        place_kernel,
        grid=(parts,),
        out_shape=(out_shape, out_shape),
        in_specs=[block] + [ANY] * len(held),
        out_specs=(out_block, out_block),
        input_output_aliases={1 + i: i for i in range(len(held))},
        compiler_params=pltpu.CompilerParams(vmem_limit_bytes=VMEM_BYTES),
        cost_estimate=pl.CostEstimate(flops=0, bytes_accessed=8 * moved.size, transcendentals=0),
        name="place",
    )(moved, *held)


def split16(value):
    high = value.astype(jnp.bfloat16)
    return high, (value - high.astype(jnp.float32)).astype(jnp.bfloat16)


def gram_kernel(ctrl, obsv, out, left, right):
    adi, cols, _, rows, lanes = ctrl.shape
    total = adi * cols

    @pl.when((pl.program_id(0) == 0) & (pl.program_id(1) == 0))
    def _():
        out[...] = jnp.zeros_like(out)

    for a in range(adi):
        left[pl.ds(a * cols * rows, cols * rows), :] = ctrl[a, :, 0].reshape(cols * rows, lanes)
        right[pl.ds(a * cols * rows, cols * rows), :] = obsv[a, :, 0].reshape(cols * rows, lanes)

    def pair(ref, row):
        values = [ref[pl.ds(row + k, total, stride=rows), :] for k in range(2)]
        return split16(jnp.concatenate(values, axis=1))

    def dot(a, b):
        return lax.dot_general(a, b, (((1,), (1,)), ((), ())), preferred_element_type=jnp.float32)

    summed = out[...]
    for row in range(0, rows, 2):
        a_high, a_low = pair(left, row)
        b_high, b_low = pair(right, row)
        summed = summed + (dot(a_high, b_high) + (dot(a_high, b_low) + dot(a_low, b_high)))
    out[...] = summed


def gram(ctrl, obsv):
    adi, cols, per, rows, lanes = ctrl.shape
    chunk = 16
    block = pl.BlockSpec((adi, cols, 1, chunk, lanes), lambda i, j: (0, 0, i, j, 0))
    total = adi * cols
    return pl.pallas_call(
        gram_kernel,
        grid=(per, rows // chunk),
        out_shape=jax.ShapeDtypeStruct((total, total), jnp.float32),
        in_specs=[block, block],
        out_specs=pl.BlockSpec((total, total), lambda i, j: (0, 0)),
        scratch_shapes=[pltpu.VMEM((total * chunk, lanes), jnp.float32)] * 2,
        compiler_params=pltpu.CompilerParams(vmem_limit_bytes=VMEM_BYTES),
        cost_estimate=pl.CostEstimate(
            flops=6 * total * total * per * rows * lanes, bytes_accessed=8 * ctrl.size, transcendentals=0
        ),
        name="gram",
    )(ctrl, obsv)


def body(input_map, output_map, region_ids, region_cond, shift_ids):
    slabs, parts = lax.axis_size("slab"), lax.axis_size("col")
    col_local, per, rows, lanes = input_map.shape
    total_x = per * slabs
    parity = lax.rem(lax.axis_index("slab"), 2)
    side = parity.reshape(1).astype(jnp.int32)
    swap = [(i, i ^ 1) for i in range(slabs)]
    upward = [(i, i + 2) for i in range(slabs - 2)]
    downward = [(i + 2, i) for i in range(slabs - 2)]

    cond_max = jnp.max(region_cond)
    shifts = 0.25 * jnp.exp2(shift_ids.astype(jnp.float32))
    scal = factor_scalars(shifts, cond_max)

    maps = [m.reshape(col_local, per * rows, lanes) for m in (input_map, output_map)]
    ids = region_ids.reshape(per * rows, lanes)
    half = col_local // 2
    width = half // GROUPS
    n = 2 * width

    def exchange(x):
        return lax.ppermute(x, "slab", swap)

    def halo(x):
        return lax.ppermute(x, "slab", upward), lax.ppermute(x, "slab", downward)

    def kept(group, out, to, first=0):
        return [(first + k, group * width, half, width, out, to + k * width) for k in range(2)]

    def sent(group, out, to, first=0, groups=1):
        return [
            (first + k, half + group * width, -half, groups * width, out, to + k * groups * width)
            for k in range(2)
        ]

    pieces = sent(0, 0, 0) + [(None, 0, 0, 1, 0, n)] + kept(0, 1, 0) + [(None, 0, 0, 1, 1, n)]
    outgoing, message = pack(side, maps, pieces, (n + 1, n + 1), ids=ids)
    got = [(exchange(outgoing), 0)]
    halos = [halo(message)]

    pieces = (
        [(0, 0, 0, n, 0, 0), (0, n, 0, 1, 0, 2 * n)] + kept(1, 0, n, 1) + sent(1, 1, 0, 1)
    )
    message, outgoing = pack(
        side, [got[0][0]] + maps, pieces, (2 * n + 1, n), after=halos[0]
    )
    got.append((exchange(outgoing), 0))
    halos.append(halo(message))

    outgoing, next_outgoing = pack(
        side, maps, sent(2, 0, 0) + sent(3, 1, 0), (n, n), after=(got[1][0],)
    )
    got.append((exchange(outgoing), 0))
    next_outgoing, _ = lax.optimization_barrier((next_outgoing, got[2][0]))
    got.append((exchange(next_outgoing), 0))

    region_float = (ids + 1).astype(jnp.float32)[None]
    held = ()
    for group in range(GROUPS):
        after = ()
        if group + 2 <= GROUPS:
            source = got[group + 1][0]
            pieces = [(0, 0, 0, n, 0, 0)]
            if group + 2 < GROUPS:
                pieces += kept(group + 2, 0, n, 1)
            count = sum(p[3] for p in pieces)
            (message,) = pack(side, [source] + maps, pieces, (count,), after=halos[-1])
            halos.append(halo(message))
            after = (message,) + tuple(got[k][0] for k in ((1, 2) if group == 0 else (group + 2,)) if k < GROUPS)
        (lo_kept, hi_kept), (lo_got, hi_got) = halos[group], halos[group + 1]
        start = 0 if group == 0 else n
        (lo_a, hi_a), (lo_b, hi_b) = halos[0], halos[1]
        pieces = [
            (lo_a, n, 0, 0, False, 0),
            (hi_a, n, 0, 2, False, 0),
            (lo_b, 2 * n, 0, 0, True, 0),
            (hi_b, 2 * n, 0, 2, True, 0),
            (region_float, 0, 0, 1, False, 0),
            (got[0][0], n, 0, 1, True, 0),
            (lo_kept, start, n, 0, False, 0),
            (hi_kept, start, n, 2, False, 0),
            (maps[0], (group * width, half), width, 1, False, 0),
            (maps[1], (group * width, half), width, 1, False, width),
            (got[group][0], 0, n, 1, True, 0),
            (lo_got, 0, n, 0, True, 0),
            (hi_got, 0, n, 2, True, 0),
        ]
        result = factors(parts, n, rows, per, side, scal, region_cond, pieces, after)
        result = result.reshape(2 * parts, *result.shape[2:])
        pairs = [[k * 2 * parts + j for j in range(2 * parts)] for k in range(slabs // 2)]
        moved = lax.all_to_all(
            result, ("slab", "col"), split_axis=0, concat_axis=0, axis_index_groups=pairs, tiled=True
        )
        held = place(group, GROUPS, moved.reshape(2, parts, *moved.shape[1:]), held)

    ctrl, obsv = (x.reshape(ADI, parts * col_local, per, rows // parts, lanes) for x in held)
    partial_value = gram(ctrl, obsv)
    count = partial_value.shape[0]
    tiles = partial_value.reshape(slabs, count // slabs, parts, count // parts).transpose(0, 2, 1, 3)
    tiles = tiles.reshape(slabs * parts, count // slabs, count // parts)
    tiles = lax.all_to_all(tiles, ("slab", "col"), split_axis=0, concat_axis=0, tiled=True)
    norm_scale = 1.0 / math.sqrt(total_x * rows * lanes)
    return (ctrl, obsv, jnp.sum(tiles, 0) * norm_scale)


def solution(mesh):
    placed = (
        P("col", "slab", None, None),
        P("col", "slab", None, None),
        P("slab", None, None),
        P(),
        P(),
    )
    return jax.shard_map(
        body,
        mesh=mesh,
        in_specs=placed,
        out_specs=(
            P(None, None, "slab", "col", None),
            P(None, None, "slab", "col", None),
            P("slab", "col"),
        ),
        check_vma=False,
    )
```

```python
import functools
import math

import jax
import jax.numpy as jnp
from jax import lax
from jax.experimental import pallas as pl
from jax.experimental.pallas import tpu as pltpu
from jax.sharding import PartitionSpec as P

ADI = 2
STEPS = 3
WIDTHS = (1, 2, 2, 2, 1)
SUB = 8
VMEM_BYTES = 50 * 1024 * 1024
ANY = pl.BlockSpec(memory_space=pl.ANY)
IN_VMEM = pl.BlockSpec(memory_space=pltpu.VMEM)
SCALARS = pl.BlockSpec(memory_space=pltpu.SMEM)


def solve_polynomial(shift_val, cond_max):
    high_eig = shift_val + 12.0 * cond_max
    mid_eig = 0.5 * (high_eig + shift_val)
    half_span = 0.5 * (high_eig - shift_val)
    ratio_eig = mid_eig / half_span
    rho_now = 1.0 / ratio_eig
    zero = jnp.zeros_like(mid_eig)
    total = [zero] * STEPS
    residual = [jnp.ones_like(mid_eig)] + [zero] * (STEPS - 1)
    direction = [1.0 / mid_eig] + [zero] * (STEPS - 1)
    for step in range(STEPS):
        total = [t + d for t, d in zip(total, direction)]
        if step < STEPS - 1:
            raised = [zero] + direction[:-1]
            residual = [r - (u + shift_val * d) for r, u, d in zip(residual, raised, direction)]
            rho_next = 1.0 / (2.0 * ratio_eig - rho_now)
            direction = [
                rho_next * rho_now * d + 2.0 * rho_next / half_span * r
                for d, r in zip(direction, residual)
            ]
            rho_now = rho_next
    return total


def factor_scalars(shifts, cond_max):
    first = solve_polynomial(shifts[0], cond_max)
    second = solve_polynomial(shifts[1], cond_max)
    scale_first = jnp.sqrt(2.0 * shifts[0])
    scale_second = jnp.sqrt(2.0 * shifts[1]) / scale_first
    both = shifts[0] + shifts[1]
    rest = [1.0 - both * second[0], -both * second[1], -both * second[2]]
    return jnp.stack([scale_first * c for c in first] + [scale_second * c for c in rest])


def pack(side, sources, pieces, counts, after=(), ids=None):
    size, lanes = sources[0].shape[1:]
    held = len(sources) + len(after) + (ids is not None)

    def kernel(*refs):
        side_ref, operands = refs[0], refs[1 : 1 + held]
        outs = refs[1 + held : 1 + held + len(counts)]
        sems = refs[-1]
        copies = []
        for k, (source, start, step, count, out, to) in enumerate(pieces):
            if source is not None:
                block = operands[source].at[pl.ds(start + step * side_ref[0], count)]
                copy = pltpu.make_async_copy(block, outs[out].at[pl.ds(to, count)], sems.at[k])
                copy.start()
                copies.append(copy)
        for source, _, _, _, out, to in pieces:
            if source is None:
                outs[out][to] = (operands[held - 1][...] + 1).astype(jnp.float32)
        for copy in copies:
            copy.wait()

    extra, specs = ([ids], [IN_VMEM]) if ids is not None else ([], [])
    moved = 4 * sum(p[3] for p in pieces) * size * lanes
    return pl.pallas_call(
        kernel,
        out_shape=[jax.ShapeDtypeStruct((c, size, lanes), jnp.float32) for c in counts],
        in_specs=[SCALARS] + [ANY] * (len(sources) + len(after)) + specs,
        out_specs=[IN_VMEM] * len(counts),
        scratch_shapes=[pltpu.SemaphoreType.DMA((len(pieces),))],
        compiler_params=pltpu.CompilerParams(vmem_limit_bytes=VMEM_BYTES),
        cost_estimate=pl.CostEstimate(flops=0, bytes_accessed=2 * moved, transcendentals=0),
        name="pack",
    )(side, *sources, *after, *extra)


def factor_kernel(spots, parts, rows, side, scal, table, *refs):
    data, (out, b, y, z, cond, dg, fx, fyn, fyp, fzn, fzp, sems) = refs[: len(spots)], refs[-12:]
    cols, size, lanes = b.shape
    window = size // rows
    per = window // 6
    own = 2 * per
    slab = per * rows
    part_rows = rows // parts
    steps = rows // SUB
    parity = side[0]

    copies = []
    for k, (start, count, block, other, to) in enumerate(spots):
        spot = 1 - parity if other else parity
        at = pl.ds(pl.multiple_of((block * 2 + spot) * slab, SUB), slab)
        if count == 0:
            copy = pltpu.make_async_copy(data[k].at[start], fx.at[at], sems.at[k])
        else:
            place_at = b.at[pl.ds(to, count), at]
            if isinstance(start, tuple):
                start = start[0] + start[1] * parity
            copy = pltpu.make_async_copy(data[k].at[pl.ds(start, count)], place_at, sems.at[k])
        copy.start()
        copies.append(copy)

    def wait(ids):
        for (_, count, *_), copy in zip(spots, copies):
            if (count == 0) == ids:
                copy.wait()

    def at(layer, r, shift=0):
        spot = layer * rows + r
        return pl.ds(spot + shift if shift else pl.multiple_of(spot, SUB), SUB)

    wait(True)
    levels = [table[k] for k in range(table.shape[0])]

    def fill(i, carry):
        r = i * SUB
        for layer in range(window):
            index = fx[at(layer, r), :]
            value = jnp.zeros_like(index)
            for k, level in enumerate(levels):
                value = jnp.where(index == float(k + 1), level, value)
            cond[at(layer, r), :] = value
        return carry

    lax.fori_loop(0, steps, fill, 0)
    row = lax.broadcasted_iota(jnp.int32, (SUB, lanes), 0)
    lane = lax.broadcasted_iota(jnp.int32, (SUB, lanes), 1)

    def prepare(i, carry):
        r = i * SUB
        below, here = cond[at(0, r), :], cond[at(1, r), :]
        fx[at(0, r), :] = jnp.where((below > 0) & (here > 0), -0.5 * (below + here), 0.0)
        for layer in range(1, window - 1):
            above = cond[at(layer + 1, r), :]
            row_n = jnp.where(row + r < rows - 1, cond[at(layer, r, 1), :], 0.0)
            row_p = jnp.where(row + r > 0, cond[at(layer, r, -1), :], 0.0)
            lane_n = jnp.where(lane < lanes - 1, pltpu.roll(here, lanes - 1, 1), 0.0)
            lane_p = jnp.where(lane > 0, pltpu.roll(here, 1, 1), 0.0)
            around = (above + below) + (row_n + row_p) + (lane_n + lane_p)
            dg[at(layer, r), :] = jnp.where(here > 0, 0.5 * (6.0 * here + around), 0.0)

            def face(other):
                return jnp.where((here > 0) & (other > 0), -0.5 * (here + other), 0.0)

            fx[at(layer, r), :] = face(above)
            fyn[at(layer, r), :] = face(row_n)
            fyp[at(layer, r), :] = face(row_p)
            fzn[at(layer, r), :] = face(lane_n)
            fzp[at(layer, r), :] = face(lane_p)
            below, here = here, above
        return carry

    lax.fori_loop(0, steps, prepare, 0)
    full = [jnp.full((SUB, lanes), scal[k], jnp.float32) for k in range(6)]
    wait(False)

    def sweep(ref, first, count, r, emit):
        below = [ref[c, at(first - 1, r), :] for c in range(cols)]
        here = [ref[c, at(first, r), :] for c in range(cols)]
        face_low = fx[at(first - 1, r), :]
        for layer in range(first, first + count):
            above = [ref[c, at(layer + 1, r), :] for c in range(cols)]
            face_high = fx[at(layer, r), :]
            diag = dg[at(layer, r), :]
            row_n, row_p = fyn[at(layer, r), :], fyp[at(layer, r), :]
            lane_n, lane_p = fzn[at(layer, r), :], fzp[at(layer, r), :]
            for c in range(cols):
                v = here[c]
                along_x = face_high * above[c] + face_low * below[c]
                along_y = row_n * ref[c, at(layer, r, 1), :] + row_p * ref[c, at(layer, r, -1), :]
                along_z = lane_n * pltpu.roll(v, lanes - 1, 1) + lane_p * pltpu.roll(v, 1, 1)
                emit(layer, c, v, (diag * v + along_x) + (along_y + along_z))
            below, here, face_low = here, above, face_high

    def store(ref, layer, c, r, value):
        ref[c, at(layer, r), :] = value

    def first_half(i, carry):
        r = i * SUB
        sweep(b, 1, window - 2, r, lambda l, c, v, a: store(y, l, c, r, full[1] * v + full[2] * a))
        return carry

    def first_end(i, carry):
        r = i * SUB
        sweep(y, 2, window - 4, r, lambda l, c, v, a: store(z, l, c, r, full[0] * b[c, at(l, r), :] + a))
        return carry

    def second_half(i, carry):
        r = i * SUB
        sweep(z, 3, window - 6, r, lambda l, c, v, a: store(y, l, c, r, full[4] * v + full[5] * a))
        return carry

    def second_end(i, carry):
        r = i * SUB
        sweep(y, own, own, r, lambda l, c, v, a: store(b, l, c, r, full[3] * z[c, at(l, r), :] + a))
        return carry

    base = len(spots)
    leaving = []

    def leave(ref, adi, part):
        for layer in range(own):
            spot = (own + layer) * rows + part * part_rows
            copy = pltpu.make_async_copy(
                ref.at[:, pl.ds(spot, part_rows)],
                out.at[layer // per, part, adi, :, layer % per],
                sems.at[base + len(leaving)],
            )
            copy.start()
            leaving.append(copy)

    lax.fori_loop(0, steps, first_half, 0)
    lax.fori_loop(0, steps, first_end, 0)
    for part in range(parts):
        leave(z, 0, part)
    lax.fori_loop(0, steps, second_half, 0)
    for part in range(parts):
        lax.fori_loop(part * steps // parts, (part + 1) * steps // parts, second_end, 0)
        leave(b, 1, part)
    for copy in leaving:
        copy.wait()


def factors(parts, cols, rows, per, side, scal, table, pieces, after):
    lanes = pieces[0][0].shape[-1]
    layers = 6 * per
    size = layers * rows
    work = cols * size * lanes
    out = (2, parts, ADI, cols, per, rows // parts, lanes)
    spots = [p[1:] for p in pieces]
    flat = pltpu.VMEM((size, lanes), jnp.float32)
    return pl.pallas_call(
        functools.partial(factor_kernel, spots, parts, rows),
        out_shape=jax.ShapeDtypeStruct(out, jnp.float32),
        in_specs=[SCALARS] * 3 + [ANY] * (len(pieces) + len(after)),
        out_specs=ANY,
        scratch_shapes=[pltpu.VMEM((cols, size, lanes), jnp.float32)] * 3
        + [flat] * 7
        + [pltpu.SemaphoreType.DMA((len(pieces) + 2 * ADI * per * parts,))],
        compiler_params=pltpu.CompilerParams(vmem_limit_bytes=VMEM_BYTES),
        cost_estimate=pl.CostEstimate(flops=40 * work, bytes_accessed=160 * work, transcendentals=0),
        name="factors",
    )(side, scal, table, *(p[0] for p in pieces), *after)


def place_kernel(moved, *refs):
    ctrl, obsv = refs[-2:]
    half = moved.shape[3] // 2
    for spot in range(2):
        for adi in range(ADI):
            ctrl[adi, 0, spot] = moved[spot, 0, adi, :half]
            obsv[adi, 0, spot] = moved[spot, 0, adi, half:]


def place(start, width, half, moved, held):
    _, parts, adi, cols, per, rows, lanes = moved.shape
    block = pl.BlockSpec((2, 1, adi, cols, per, rows, lanes), lambda i: (0, i, 0, 0, 0, 0, 0))
    out_block = pl.BlockSpec(
        (adi, 1, 2, width, per, rows, lanes), lambda i: (0, i, 0, start // width, 0, 0, 0)
    )
    out_shape = jax.ShapeDtypeStruct((adi, parts, 2, half, per, rows, lanes), jnp.float32)
    return pl.pallas_call(
        place_kernel,
        grid=(parts,),
        out_shape=(out_shape, out_shape),
        in_specs=[block] + [ANY] * len(held),
        out_specs=(out_block, out_block),
        input_output_aliases={1 + i: i for i in range(len(held))},
        compiler_params=pltpu.CompilerParams(vmem_limit_bytes=VMEM_BYTES),
        cost_estimate=pl.CostEstimate(flops=0, bytes_accessed=8 * moved.size, transcendentals=0),
        name="place",
    )(moved, *held)


def split16(value):
    high = value.astype(jnp.bfloat16)
    return high, (value - high.astype(jnp.float32)).astype(jnp.bfloat16)


def gram_kernel(ctrl, obsv, out, left, right):
    adi, cols, _, rows, lanes = ctrl.shape
    total = adi * cols

    @pl.when((pl.program_id(0) == 0) & (pl.program_id(1) == 0))
    def _():
        out[...] = jnp.zeros_like(out)

    for a in range(adi):
        left[pl.ds(a * cols * rows, cols * rows), :] = ctrl[a, :, 0].reshape(cols * rows, lanes)
        right[pl.ds(a * cols * rows, cols * rows), :] = obsv[a, :, 0].reshape(cols * rows, lanes)

    def pair(ref, row):
        values = [ref[pl.ds(row + k, total, stride=rows), :] for k in range(2)]
        return split16(jnp.concatenate(values, axis=1))

    def dot(a, b):
        return lax.dot_general(a, b, (((1,), (1,)), ((), ())), preferred_element_type=jnp.float32)

    summed = out[...]
    for row in range(0, rows, 2):
        a_high, a_low = pair(left, row)
        b_high, b_low = pair(right, row)
        summed = summed + (dot(a_high, b_high) + (dot(a_high, b_low) + dot(a_low, b_high)))
    out[...] = summed


def gram(ctrl, obsv):
    adi, cols, per, rows, lanes = ctrl.shape
    chunk = 16
    block = pl.BlockSpec((adi, cols, 1, chunk, lanes), lambda i, j: (0, 0, i, j, 0))
    total = adi * cols
    return pl.pallas_call(
        gram_kernel,
        grid=(per, rows // chunk),
        out_shape=jax.ShapeDtypeStruct((total, total), jnp.float32),
        in_specs=[block, block],
        out_specs=pl.BlockSpec((total, total), lambda i, j: (0, 0)),
        scratch_shapes=[pltpu.VMEM((total * chunk, lanes), jnp.float32)] * 2,
        compiler_params=pltpu.CompilerParams(vmem_limit_bytes=VMEM_BYTES),
        cost_estimate=pl.CostEstimate(
            flops=6 * total * total * per * rows * lanes, bytes_accessed=8 * ctrl.size, transcendentals=0
        ),
        name="gram",
    )(ctrl, obsv)


def body(input_map, output_map, region_ids, region_cond, shift_ids):
    slabs, parts = lax.axis_size("slab"), lax.axis_size("col")
    col_local, per, rows, lanes = input_map.shape
    total_x = per * slabs
    parity = lax.rem(lax.axis_index("slab"), 2)
    side = parity.reshape(1).astype(jnp.int32)
    swap = [(i, i ^ 1) for i in range(slabs)]
    upward = [(i, i + 2) for i in range(slabs - 2)]
    downward = [(i + 2, i) for i in range(slabs - 2)]

    cond_max = jnp.max(region_cond)
    shifts = 0.25 * jnp.exp2(shift_ids.astype(jnp.float32))
    scal = factor_scalars(shifts, cond_max)

    maps = [m.reshape(col_local, per * rows, lanes) for m in (input_map, output_map)]
    ids = region_ids.reshape(per * rows, lanes)
    half = col_local // 2
    unit = half // sum(WIDTHS)
    widths = [unit * w for w in WIDTHS]
    total = len(widths)
    order = sorted(range(total), key=lambda g: (-widths[g], g))
    starts = [sum(widths[h] for h in order[: order.index(g)]) for g in range(total)]
    counts = [2 * w for w in widths]

    def exchange(x):
        return lax.ppermute(x, "slab", swap)

    def kept(group, out, to, first=0):
        w = widths[group]
        return [(first + k, starts[group], half, w, out, to + k * w) for k in range(2)]

    def sent(group, out, to, first=0):
        w = widths[group]
        return [(first + k, half + starts[group], -half, w, out, to + k * w) for k in range(2)]

    got, halos = {}, []

    def halo(message):
        up = down = message
        if halos:
            up, lo = lax.optimization_barrier((message, halos[-1][0]))
            down, hi = lax.optimization_barrier((message, halos[-1][1]))
            halos[-1] = (lo, hi)
        halos.append((lax.ppermute(up, "slab", upward), lax.ppermute(down, "slab", downward)))

    n = counts[0]
    pieces = sent(0, 0, 0) + [(None, 0, 0, 1, 0, n)] + kept(0, 1, 0) + [(None, 0, 0, 1, 1, n)]
    outgoing, message = pack(side, maps, pieces, (n + 1, n + 1), ids=ids)
    got[0] = (exchange(outgoing), 0)
    halo(message)

    m = counts[1]
    pieces = [(0, 0, 0, n, 0, 0), (0, n, 0, 1, 0, n + m)] + kept(1, 0, n, 1) + sent(1, 1, 0, 1)
    message, outgoing = pack(
        side, [got[0][0]] + maps, pieces, (n + m + 1, m), after=halos[0]
    )
    halo(message)
    got[1] = (exchange(outgoing), 0)

    (first, later) = pack(
        side,
        maps,
        sent(2, 0, 0) + sent(3, 1, 0) + sent(4, 1, counts[3]),
        (counts[2], counts[3] + counts[4]),
        after=(got[1][0],),
    )
    got[2] = (exchange(first), 0)
    later, waited = lax.optimization_barrier((later, got[2][0]))
    got[2] = (waited, 0)
    got[3] = (exchange(later), 0)
    got[4] = (got[3][0], counts[3])

    region_float = (ids + 1).astype(jnp.float32)[None]
    held = ()
    for group in range(total):
        n = counts[group]
        after = ()
        if group + 1 < total:
            source, begin = got[group + 1]
            m = counts[group + 1]
            pieces = [(0, begin, 0, m, 0, 0)]
            if group + 2 < total:
                pieces += kept(group + 2, 0, m, 1)
            count = sum(p[3] for p in pieces)
            (message,) = pack(side, [source] + maps, pieces, (count,))
            halo(message)
            after = (message, got[2][0])
        (lo_kept, hi_kept), (lo_got, hi_got) = halos[group], halos[group + 1]
        before = counts[group - 1] if group else 0
        (lo_a, hi_a), (lo_b, hi_b) = halos[0], halos[1]
        pieces = [
            (lo_a, counts[0], 0, 0, False, 0),
            (hi_a, counts[0], 0, 2, False, 0),
            (lo_b, counts[0] + counts[1], 0, 0, True, 0),
            (hi_b, counts[0] + counts[1], 0, 2, True, 0),
            (region_float, 0, 0, 1, False, 0),
            (got[0][0], counts[0], 0, 1, True, 0),
            (lo_kept, before, n, 0, False, 0),
            (hi_kept, before, n, 2, False, 0),
            (maps[0], (starts[group], half), n // 2, 1, False, 0),
            (maps[1], (starts[group], half), n // 2, 1, False, n // 2),
            (got[group][0], got[group][1], n, 1, True, 0),
            (lo_got, 0, n, 0, True, 0),
            (hi_got, 0, n, 2, True, 0),
        ]
        result = factors(parts, n, rows, per, side, scal, region_cond, pieces, after)
        result = result.reshape(2 * parts, *result.shape[2:])
        pairs = [[k * 2 * parts + j for j in range(2 * parts)] for k in range(slabs // 2)]
        moved = lax.all_to_all(
            result, ("slab", "col"), split_axis=0, concat_axis=0, axis_index_groups=pairs, tiled=True
        )
        moved = moved.reshape(2, parts, *moved.shape[1:])
        held = place(starts[group], widths[group], half, moved, held)

    ctrl, obsv = (x.reshape(ADI, parts * col_local, per, rows // parts, lanes) for x in held)
    partial_value = gram(ctrl, obsv)
    count = partial_value.shape[0]
    tiles = partial_value.reshape(slabs, count // slabs, parts, count // parts).transpose(0, 2, 1, 3)
    tiles = tiles.reshape(slabs * parts, count // slabs, count // parts)
    tiles = lax.all_to_all(tiles, ("slab", "col"), split_axis=0, concat_axis=0, tiled=True)
    norm_scale = 1.0 / math.sqrt(total_x * rows * lanes)
    return (ctrl, obsv, jnp.sum(tiles, 0) * norm_scale)


def solution(mesh):
    placed = (
        P("col", "slab", None, None),
        P("col", "slab", None, None),
        P("slab", None, None),
        P(),
        P(),
    )
    return jax.shard_map(
        body,
        mesh=mesh,
        in_specs=placed,
        out_specs=(
            P(None, None, "slab", "col", None),
            P(None, None, "slab", "col", None),
            P("slab", "col"),
        ),
        check_vma=False,
    )
```

```python
import functools
import math

import jax
import jax.numpy as jnp
from jax import lax
from jax.experimental import pallas as pl
from jax.experimental.pallas import tpu as pltpu
from jax.sharding import PartitionSpec as P

ADI = 2
STEPS = 3
WIDTHS = (1, 2, 2, 2, 1)
SUB = 8
VMEM_BYTES = 50 * 1024 * 1024
ANY = pl.BlockSpec(memory_space=pl.ANY)
IN_VMEM = pl.BlockSpec(memory_space=pltpu.VMEM)
SCALARS = pl.BlockSpec(memory_space=pltpu.SMEM)


def solve_polynomial(shift_val, cond_max):
    high_eig = shift_val + 12.0 * cond_max
    mid_eig = 0.5 * (high_eig + shift_val)
    half_span = 0.5 * (high_eig - shift_val)
    ratio_eig = mid_eig / half_span
    rho_now = 1.0 / ratio_eig
    zero = jnp.zeros_like(mid_eig)
    total = [zero] * STEPS
    residual = [jnp.ones_like(mid_eig)] + [zero] * (STEPS - 1)
    direction = [1.0 / mid_eig] + [zero] * (STEPS - 1)
    for step in range(STEPS):
        total = [t + d for t, d in zip(total, direction)]
        if step < STEPS - 1:
            raised = [zero] + direction[:-1]
            residual = [r - (u + shift_val * d) for r, u, d in zip(residual, raised, direction)]
            rho_next = 1.0 / (2.0 * ratio_eig - rho_now)
            direction = [
                rho_next * rho_now * d + 2.0 * rho_next / half_span * r
                for d, r in zip(direction, residual)
            ]
            rho_now = rho_next
    return total


def factor_scalars(shifts, cond_max):
    first = solve_polynomial(shifts[0], cond_max)
    second = solve_polynomial(shifts[1], cond_max)
    scale_first = jnp.sqrt(2.0 * shifts[0])
    scale_second = jnp.sqrt(2.0 * shifts[1]) / scale_first
    both = shifts[0] + shifts[1]
    rest = [1.0 - both * second[0], -both * second[1], -both * second[2]]
    return jnp.stack([scale_first * c for c in first] + [scale_second * c for c in rest])


def pack(side, sources, pieces, counts, after=(), ids=None):
    size, lanes = sources[0].shape[1:]
    held = len(sources) + len(after) + (ids is not None)

    def kernel(*refs):
        side_ref, operands = refs[0], refs[1 : 1 + held]
        outs = refs[1 + held : 1 + held + len(counts)]
        sems = refs[-1]
        copies = []
        for k, (source, start, step, count, out, to) in enumerate(pieces):
            if source is not None:
                block = operands[source].at[pl.ds(start + step * side_ref[0], count)]
                copy = pltpu.make_async_copy(block, outs[out].at[pl.ds(to, count)], sems.at[k])
                copy.start()
                copies.append(copy)
        for source, _, _, _, out, to in pieces:
            if source is None:
                outs[out][to] = (operands[held - 1][...] + 1).astype(jnp.float32)
        for copy in copies:
            copy.wait()

    extra, specs = ([ids], [IN_VMEM]) if ids is not None else ([], [])
    moved = 4 * sum(p[3] for p in pieces) * size * lanes
    return pl.pallas_call(
        kernel,
        out_shape=[jax.ShapeDtypeStruct((c, size, lanes), jnp.float32) for c in counts],
        in_specs=[SCALARS] + [ANY] * (len(sources) + len(after)) + specs,
        out_specs=[IN_VMEM] * len(counts),
        scratch_shapes=[pltpu.SemaphoreType.DMA((len(pieces),))],
        compiler_params=pltpu.CompilerParams(vmem_limit_bytes=VMEM_BYTES),
        cost_estimate=pl.CostEstimate(flops=0, bytes_accessed=2 * moved, transcendentals=0),
        name="pack",
    )(side, *sources, *after, *extra)


def factor_kernel(spots, parts, rows, side, scal, table, *refs):
    data, (out, b, y, z, cond, dg, fx, fyn, fyp, fzn, fzp, sems) = refs[: len(spots)], refs[-12:]
    cols, size, lanes = b.shape
    window = size // rows
    per = window // 6
    own = 2 * per
    slab = per * rows
    part_rows = rows // parts
    steps = rows // SUB
    parity = side[0]

    copies = []
    for k, (start, count, block, other, to) in enumerate(spots):
        spot = 1 - parity if other else parity
        at = pl.ds(pl.multiple_of((block * 2 + spot) * slab, SUB), slab)
        if count == 0:
            copy = pltpu.make_async_copy(data[k].at[start], fx.at[at], sems.at[k])
        else:
            place_at = b.at[pl.ds(to, count), at]
            if isinstance(start, tuple):
                start = start[0] + start[1] * parity
            copy = pltpu.make_async_copy(data[k].at[pl.ds(start, count)], place_at, sems.at[k])
        copy.start()
        copies.append(copy)

    def wait(ids):
        for (_, count, *_), copy in zip(spots, copies):
            if (count == 0) == ids:
                copy.wait()

    def at(layer, r, shift=0):
        spot = layer * rows + r
        return pl.ds(spot + shift if shift else pl.multiple_of(spot, SUB), SUB)

    def repeat(first, last, times, body):
        while (last - first) % times:
            times -= 1

        def turn(i, carry):
            for k in range(times):
                body(first + i * times + k)
            return carry

        lax.fori_loop(0, (last - first) // times, turn, 0)

    wait(True)
    levels = [table[k] for k in range(table.shape[0])]

    def fill(i):
        r = i * SUB
        for layer in range(window):
            index = fx[at(layer, r), :]
            value = jnp.zeros_like(index)
            for k, level in enumerate(levels):
                value = jnp.where(index == float(k + 1), level, value)
            cond[at(layer, r), :] = value

    repeat(0, steps, 4, fill)
    row = lax.broadcasted_iota(jnp.int32, (SUB, lanes), 0)
    lane = lax.broadcasted_iota(jnp.int32, (SUB, lanes), 1)

    def prepare(i):
        r = i * SUB
        below, here = cond[at(0, r), :], cond[at(1, r), :]
        fx[at(0, r), :] = jnp.where((below > 0) & (here > 0), -0.5 * (below + here), 0.0)
        for layer in range(1, window - 1):
            above = cond[at(layer + 1, r), :]
            row_n = jnp.where(row + r < rows - 1, cond[at(layer, r, 1), :], 0.0)
            row_p = jnp.where(row + r > 0, cond[at(layer, r, -1), :], 0.0)
            lane_n = jnp.where(lane < lanes - 1, pltpu.roll(here, lanes - 1, 1), 0.0)
            lane_p = jnp.where(lane > 0, pltpu.roll(here, 1, 1), 0.0)
            around = (above + below) + (row_n + row_p) + (lane_n + lane_p)
            dg[at(layer, r), :] = jnp.where(here > 0, 0.5 * (6.0 * here + around), 0.0)

            def face(other):
                return jnp.where((here > 0) & (other > 0), -0.5 * (here + other), 0.0)

            fx[at(layer, r), :] = face(above)
            fyn[at(layer, r), :] = face(row_n)
            fyp[at(layer, r), :] = face(row_p)
            fzn[at(layer, r), :] = face(lane_n)
            fzp[at(layer, r), :] = face(lane_p)
            below, here = here, above

    repeat(0, steps, 2, prepare)
    full = [jnp.full((SUB, lanes), scal[k], jnp.float32) for k in range(6)]
    wait(False)

    def sweep(ref, first, count, r, emit):
        below = [ref[c, at(first - 1, r), :] for c in range(cols)]
        here = [ref[c, at(first, r), :] for c in range(cols)]
        face_low = fx[at(first - 1, r), :]
        for layer in range(first, first + count):
            above = [ref[c, at(layer + 1, r), :] for c in range(cols)]
            face_high = fx[at(layer, r), :]
            diag = dg[at(layer, r), :]
            row_n, row_p = fyn[at(layer, r), :], fyp[at(layer, r), :]
            lane_n, lane_p = fzn[at(layer, r), :], fzp[at(layer, r), :]
            for c in range(cols):
                v = here[c]
                along_x = face_high * above[c] + face_low * below[c]
                along_y = row_n * ref[c, at(layer, r, 1), :] + row_p * ref[c, at(layer, r, -1), :]
                along_z = lane_n * pltpu.roll(v, lanes - 1, 1) + lane_p * pltpu.roll(v, 1, 1)
                emit(layer, c, v, (diag * v + along_x) + (along_y + along_z))
            below, here, face_low = here, above, face_high

    def store(ref, layer, c, r, value):
        ref[c, at(layer, r), :] = value

    def first_half(i):
        r = i * SUB
        sweep(b, 1, window - 2, r, lambda l, c, v, a: store(y, l, c, r, full[1] * v + full[2] * a))

    def first_end(i):
        r = i * SUB
        sweep(y, 2, window - 4, r, lambda l, c, v, a: store(z, l, c, r, full[0] * b[c, at(l, r), :] + a))

    def second_half(i):
        r = i * SUB
        sweep(z, 3, window - 6, r, lambda l, c, v, a: store(y, l, c, r, full[4] * v + full[5] * a))

    def second_end(i):
        r = i * SUB
        sweep(y, own, own, r, lambda l, c, v, a: store(b, l, c, r, full[3] * z[c, at(l, r), :] + a))

    base = len(spots)
    leaving = []

    def leave(ref, adi, part):
        for layer in range(own):
            spot = (own + layer) * rows + part * part_rows
            copy = pltpu.make_async_copy(
                ref.at[:, pl.ds(spot, part_rows)],
                out.at[layer // per, part, adi, :, layer % per],
                sems.at[base + len(leaving)],
            )
            copy.start()
            leaving.append(copy)

    repeat(0, steps, 2, first_half)
    repeat(0, steps, 2, first_end)
    for part in range(parts):
        leave(z, 0, part)
    repeat(0, steps, 3, second_half)
    for part in range(parts):
        repeat(part * steps // parts, (part + 1) * steps // parts, 3, second_end)
        leave(b, 1, part)
    for copy in leaving:
        copy.wait()


def factors(parts, cols, rows, per, side, scal, table, pieces, after):
    lanes = pieces[0][0].shape[-1]
    layers = 6 * per
    size = layers * rows
    work = cols * size * lanes
    out = (2, parts, ADI, cols, per, rows // parts, lanes)
    spots = [p[1:] for p in pieces]
    flat = pltpu.VMEM((size, lanes), jnp.float32)
    return pl.pallas_call(
        functools.partial(factor_kernel, spots, parts, rows),
        out_shape=jax.ShapeDtypeStruct(out, jnp.float32),
        in_specs=[SCALARS] * 3 + [ANY] * (len(pieces) + len(after)),
        out_specs=ANY,
        scratch_shapes=[pltpu.VMEM((cols, size, lanes), jnp.float32)] * 3
        + [flat] * 7
        + [pltpu.SemaphoreType.DMA((len(pieces) + 2 * ADI * per * parts,))],
        compiler_params=pltpu.CompilerParams(vmem_limit_bytes=VMEM_BYTES),
        cost_estimate=pl.CostEstimate(flops=40 * work, bytes_accessed=480 * work, transcendentals=0),
        name="factors",
    )(side, scal, table, *(p[0] for p in pieces), *after)


def place_kernel(moved, *refs):
    ctrl, obsv = refs[-2:]
    half = moved.shape[3] // 2
    for spot in range(2):
        for adi in range(ADI):
            ctrl[adi, 0, spot] = moved[spot, 0, adi, :half]
            obsv[adi, 0, spot] = moved[spot, 0, adi, half:]


def place(start, width, half, moved, held):
    _, parts, adi, cols, per, rows, lanes = moved.shape
    block = pl.BlockSpec((2, 1, adi, cols, per, rows, lanes), lambda i: (0, i, 0, 0, 0, 0, 0))
    out_block = pl.BlockSpec(
        (adi, 1, 2, width, per, rows, lanes), lambda i: (0, i, 0, start // width, 0, 0, 0)
    )
    out_shape = jax.ShapeDtypeStruct((adi, parts, 2, half, per, rows, lanes), jnp.float32)
    return pl.pallas_call(
        place_kernel,
        grid=(parts,),
        out_shape=(out_shape, out_shape),
        in_specs=[block] + [ANY] * len(held),
        out_specs=(out_block, out_block),
        input_output_aliases={1 + i: i for i in range(len(held))},
        compiler_params=pltpu.CompilerParams(vmem_limit_bytes=VMEM_BYTES),
        cost_estimate=pl.CostEstimate(flops=0, bytes_accessed=8 * moved.size, transcendentals=0),
        name="place",
    )(moved, *held)


def split16(value):
    high = value.astype(jnp.bfloat16)
    return high, (value - high.astype(jnp.float32)).astype(jnp.bfloat16)


def gram_kernel(ctrl, obsv, out, left, right):
    adi, cols, _, rows, lanes = ctrl.shape
    total = adi * cols

    @pl.when((pl.program_id(0) == 0) & (pl.program_id(1) == 0))
    def _():
        out[...] = jnp.zeros_like(out)

    for a in range(adi):
        left[pl.ds(a * cols * rows, cols * rows), :] = ctrl[a, :, 0].reshape(cols * rows, lanes)
        right[pl.ds(a * cols * rows, cols * rows), :] = obsv[a, :, 0].reshape(cols * rows, lanes)

    def pair(ref, row):
        values = [ref[pl.ds(row + k, total, stride=rows), :] for k in range(2)]
        return split16(jnp.concatenate(values, axis=1))

    def dot(a, b):
        return lax.dot_general(a, b, (((1,), (1,)), ((), ())), preferred_element_type=jnp.float32)

    summed = out[...]
    for row in range(0, rows, 2):
        a_high, a_low = pair(left, row)
        b_high, b_low = pair(right, row)
        summed = summed + (dot(a_high, b_high) + (dot(a_high, b_low) + dot(a_low, b_high)))
    out[...] = summed


def gram(ctrl, obsv):
    adi, cols, per, rows, lanes = ctrl.shape
    chunk = 16
    block = pl.BlockSpec((adi, cols, 1, chunk, lanes), lambda i, j: (0, 0, i, j, 0))
    total = adi * cols
    return pl.pallas_call(
        gram_kernel,
        grid=(per, rows // chunk),
        out_shape=jax.ShapeDtypeStruct((total, total), jnp.float32),
        in_specs=[block, block],
        out_specs=pl.BlockSpec((total, total), lambda i, j: (0, 0)),
        scratch_shapes=[pltpu.VMEM((total * chunk, lanes), jnp.float32)] * 2,
        compiler_params=pltpu.CompilerParams(vmem_limit_bytes=VMEM_BYTES),
        cost_estimate=pl.CostEstimate(
            flops=6 * total * total * per * rows * lanes, bytes_accessed=8 * ctrl.size, transcendentals=0
        ),
        name="gram",
    )(ctrl, obsv)


def body(input_map, output_map, region_ids, region_cond, shift_ids):
    slabs, parts = lax.axis_size("slab"), lax.axis_size("col")
    col_local, per, rows, lanes = input_map.shape
    total_x = per * slabs
    parity = lax.rem(lax.axis_index("slab"), 2)
    side = parity.reshape(1).astype(jnp.int32)
    swap = [(i, i ^ 1) for i in range(slabs)]
    upward = [(i, i + 2) for i in range(slabs - 2)]
    downward = [(i + 2, i) for i in range(slabs - 2)]

    cond_max = jnp.max(region_cond)
    shifts = 0.25 * jnp.exp2(shift_ids.astype(jnp.float32))
    scal = factor_scalars(shifts, cond_max)

    maps = [m.reshape(col_local, per * rows, lanes) for m in (input_map, output_map)]
    ids = region_ids.reshape(per * rows, lanes)
    half = col_local // 2
    unit = half // sum(WIDTHS)
    widths = [unit * w for w in WIDTHS]
    total = len(widths)
    order = sorted(range(total), key=lambda g: (-widths[g], g))
    starts = [sum(widths[h] for h in order[: order.index(g)]) for g in range(total)]
    counts = [2 * w for w in widths]

    def exchange(x):
        return lax.ppermute(x, "slab", swap)

    def kept(group, out, to, first=0):
        w = widths[group]
        return [(first + k, starts[group], half, w, out, to + k * w) for k in range(2)]

    def sent(group, out, to, first=0):
        w = widths[group]
        return [(first + k, half + starts[group], -half, w, out, to + k * w) for k in range(2)]

    got, halos = {}, []

    def halo(message):
        up = down = message
        if halos:
            up, lo = lax.optimization_barrier((message, halos[-1][0]))
            down, hi = lax.optimization_barrier((message, halos[-1][1]))
            halos[-1] = (lo, hi)
        halos.append((lax.ppermute(up, "slab", upward), lax.ppermute(down, "slab", downward)))

    n = counts[0]
    pieces = sent(0, 0, 0) + [(None, 0, 0, 1, 0, n)] + kept(0, 1, 0) + [(None, 0, 0, 1, 1, n)]
    outgoing, message = pack(side, maps, pieces, (n + 1, n + 1), ids=ids)
    got[0] = (exchange(outgoing), 0)
    halo(message)

    m = counts[1]
    pieces = [(0, 0, 0, n, 0, 0), (0, n, 0, 1, 0, n + m)] + kept(1, 0, n, 1) + sent(1, 1, 0, 1)
    message, outgoing = pack(
        side, [got[0][0]] + maps, pieces, (n + m + 1, m), after=halos[0]
    )
    halo(message)
    got[1] = (exchange(outgoing), 0)

    begins = [sum(counts[2:g]) for g in range(total)]
    pieces = [(0, 0, 0, m, 1, 0)] + kept(2, 1, m, 1)
    for g in range(2, total):
        pieces += sent(g, 0, begins[g], 1)
    outgoing, message = pack(
        side, [got[1][0]] + maps, pieces, (sum(counts[2:]), m + counts[2])
    )
    rest = exchange(outgoing)
    halo(message)
    pieces = []
    for g in range(2, total):
        got[g] = (rest, begins[g])
        pieces.append((0, begins[g], 0, counts[g], g - 2, 0))
        if g + 1 < total:
            pieces += kept(g + 1, g - 2, counts[g], 1)
    lengths = [counts[g] + (counts[g + 1] if g + 1 < total else 0) for g in range(2, total)]
    messages = pack(side, [rest] + maps, pieces, lengths)

    region_float = (ids + 1).astype(jnp.float32)[None]
    held = ()
    for group in range(total):
        n = counts[group]
        if 0 < group < total - 1:
            halo(messages[group - 1])
        after = messages if group == 0 else ()
        (lo_kept, hi_kept), (lo_got, hi_got) = halos[group], halos[group + 1]
        before = counts[group - 1] if group else 0
        (lo_a, hi_a), (lo_b, hi_b) = halos[0], halos[1]
        pieces = [
            (lo_a, counts[0], 0, 0, False, 0),
            (hi_a, counts[0], 0, 2, False, 0),
            (lo_b, counts[0] + counts[1], 0, 0, True, 0),
            (hi_b, counts[0] + counts[1], 0, 2, True, 0),
            (region_float, 0, 0, 1, False, 0),
            (got[0][0], counts[0], 0, 1, True, 0),
            (lo_kept, before, n, 0, False, 0),
            (hi_kept, before, n, 2, False, 0),
            (maps[0], (starts[group], half), n // 2, 1, False, 0),
            (maps[1], (starts[group], half), n // 2, 1, False, n // 2),
            (got[group][0], got[group][1], n, 1, True, 0),
            (lo_got, 0, n, 0, True, 0),
            (hi_got, 0, n, 2, True, 0),
        ]
        result = factors(parts, n, rows, per, side, scal, region_cond, pieces, after)
        result = result.reshape(2 * parts, *result.shape[2:])
        pairs = [[k * 2 * parts + j for j in range(2 * parts)] for k in range(slabs // 2)]
        moved = lax.all_to_all(
            result, ("slab", "col"), split_axis=0, concat_axis=0, axis_index_groups=pairs, tiled=True
        )
        moved = moved.reshape(2, parts, *moved.shape[1:])
        held = place(starts[group], widths[group], half, moved, held)

    ctrl, obsv = (x.reshape(ADI, parts * col_local, per, rows // parts, lanes) for x in held)
    partial_value = gram(ctrl, obsv)
    count = partial_value.shape[0]
    tiles = partial_value.reshape(slabs, count // slabs, parts, count // parts).transpose(0, 2, 1, 3)
    tiles = tiles.reshape(slabs * parts, count // slabs, count // parts)
    tiles = lax.all_to_all(tiles, ("slab", "col"), split_axis=0, concat_axis=0, tiled=True)
    norm_scale = 1.0 / math.sqrt(total_x * rows * lanes)
    return (ctrl, obsv, jnp.sum(tiles, 0) * norm_scale)


def solution(mesh):
    placed = (
        P("col", "slab", None, None),
        P("col", "slab", None, None),
        P("slab", None, None),
        P(),
        P(),
    )
    return jax.shard_map(
        body,
        mesh=mesh,
        in_specs=placed,
        out_specs=(
            P(None, None, "slab", "col", None),
            P(None, None, "slab", "col", None),
            P("slab", "col"),
        ),
        check_vma=False,
    )
```

```python
import functools
import math

import jax
import jax.numpy as jnp
from jax import lax
from jax.experimental import pallas as pl
from jax.experimental.pallas import tpu as pltpu
from jax.sharding import PartitionSpec as P

ADI = 2
STEPS = 3
WIDTHS = (1, 2, 2, 2, 1)
SUB = 8
VMEM_BYTES = 50 * 1024 * 1024
ANY = pl.BlockSpec(memory_space=pl.ANY)
IN_VMEM = pl.BlockSpec(memory_space=pltpu.VMEM)
SCALARS = pl.BlockSpec(memory_space=pltpu.SMEM)


def solve_polynomial(shift_val, cond_max):
    high_eig = shift_val + 12.0 * cond_max
    mid_eig = 0.5 * (high_eig + shift_val)
    half_span = 0.5 * (high_eig - shift_val)
    ratio_eig = mid_eig / half_span
    rho_now = 1.0 / ratio_eig
    zero = jnp.zeros_like(mid_eig)
    total = [zero] * STEPS
    residual = [jnp.ones_like(mid_eig)] + [zero] * (STEPS - 1)
    direction = [1.0 / mid_eig] + [zero] * (STEPS - 1)
    for step in range(STEPS):
        total = [t + d for t, d in zip(total, direction)]
        if step < STEPS - 1:
            raised = [zero] + direction[:-1]
            residual = [r - (u + shift_val * d) for r, u, d in zip(residual, raised, direction)]
            rho_next = 1.0 / (2.0 * ratio_eig - rho_now)
            direction = [
                rho_next * rho_now * d + 2.0 * rho_next / half_span * r
                for d, r in zip(direction, residual)
            ]
            rho_now = rho_next
    return total


def factor_scalars(shifts, cond_max):
    first = solve_polynomial(shifts[0], cond_max)
    second = solve_polynomial(shifts[1], cond_max)
    scale_first = jnp.sqrt(2.0 * shifts[0])
    scale_second = jnp.sqrt(2.0 * shifts[1]) / scale_first
    both = shifts[0] + shifts[1]
    rest = [1.0 - both * second[0], -both * second[1], -both * second[2]]
    return jnp.stack([scale_first * c for c in first] + [scale_second * c for c in rest])


def pack(side, sources, pieces, counts, after=(), ids=None):
    size, lanes = sources[0].shape[1:]
    held = len(sources) + len(after) + (ids is not None)

    def kernel(*refs):
        side_ref, operands = refs[0], refs[1 : 1 + held]
        outs = refs[1 + held : 1 + held + len(counts)]
        sems = refs[-1]
        copies = []
        for k, (source, start, step, count, out, to) in enumerate(pieces):
            if source is not None:
                block = operands[source].at[pl.ds(start + step * side_ref[0], count)]
                copy = pltpu.make_async_copy(block, outs[out].at[pl.ds(to, count)], sems.at[k])
                copy.start()
                copies.append(copy)
        for source, _, _, _, out, to in pieces:
            if source is None:
                outs[out][to] = (operands[held - 1][...] + 1).astype(jnp.float32)
        for copy in copies:
            copy.wait()

    extra, specs = ([ids], [IN_VMEM]) if ids is not None else ([], [])
    moved = 4 * sum(p[3] for p in pieces) * size * lanes
    return pl.pallas_call(
        kernel,
        out_shape=[jax.ShapeDtypeStruct((c, size, lanes), jnp.float32) for c in counts],
        in_specs=[SCALARS] + [ANY] * (len(sources) + len(after)) + specs,
        out_specs=[IN_VMEM] * len(counts),
        scratch_shapes=[pltpu.SemaphoreType.DMA((len(pieces),))],
        compiler_params=pltpu.CompilerParams(vmem_limit_bytes=VMEM_BYTES),
        cost_estimate=pl.CostEstimate(flops=0, bytes_accessed=2 * moved, transcendentals=0),
        name="pack",
    )(side, *sources, *after, *extra)


def factor_kernel(spots, parts, rows, side, scal, table, *refs):
    data, (out, b, y, z, cond, dg, fx, fyn, fyp, fzn, fzp, sems) = refs[: len(spots)], refs[-12:]
    cols, size, lanes = b.shape
    window = size // rows
    per = window // 6
    own = 2 * per
    slab = per * rows
    part_rows = rows // parts
    steps = rows // SUB
    parity = side[0]

    copies = []
    for k, (start, count, block, other, to) in enumerate(spots):
        spot = 1 - parity if other else parity
        at = pl.ds(pl.multiple_of((block * 2 + spot) * slab, SUB), slab)
        if count == 0:
            copy = pltpu.make_async_copy(data[k].at[start], fx.at[at], sems.at[k])
        else:
            place_at = b.at[pl.ds(to, count), at]
            if isinstance(start, tuple):
                start = start[0] + start[1] * parity
            copy = pltpu.make_async_copy(data[k].at[pl.ds(start, count)], place_at, sems.at[k])
        copy.start()
        copies.append(copy)

    def wait(ids):
        for (_, count, *_), copy in zip(spots, copies):
            if (count == 0) == ids:
                copy.wait()

    def at(layer, r, shift=0):
        spot = layer * rows + r
        return pl.ds(spot + shift if shift else pl.multiple_of(spot, SUB), SUB)

    def repeat(first, last, times, body):
        while (last - first) % times:
            times -= 1

        def turn(i, carry):
            for k in range(times):
                body(first + i * times + k)
            return carry

        lax.fori_loop(0, (last - first) // times, turn, 0)

    wait(True)
    levels = [table[k] for k in range(table.shape[0])]

    def fill(i):
        r = i * SUB
        for layer in range(window):
            index = fx[at(layer, r), :]
            value = jnp.zeros_like(index)
            for k, level in enumerate(levels):
                value = jnp.where(index == float(k + 1), level, value)
            cond[at(layer, r), :] = value

    repeat(0, steps, 4, fill)
    row = lax.broadcasted_iota(jnp.int32, (SUB, lanes), 0)
    lane = lax.broadcasted_iota(jnp.int32, (SUB, lanes), 1)

    def prepare(i):
        r = i * SUB
        below, here = cond[at(0, r), :], cond[at(1, r), :]
        fx[at(0, r), :] = jnp.where((below > 0) & (here > 0), -0.5 * (below + here), 0.0)
        for layer in range(1, window - 1):
            above = cond[at(layer + 1, r), :]
            row_n = jnp.where(row + r < rows - 1, cond[at(layer, r, 1), :], 0.0)
            row_p = jnp.where(row + r > 0, cond[at(layer, r, -1), :], 0.0)
            lane_n = jnp.where(lane < lanes - 1, pltpu.roll(here, lanes - 1, 1), 0.0)
            lane_p = jnp.where(lane > 0, pltpu.roll(here, 1, 1), 0.0)
            around = (above + below) + (row_n + row_p) + (lane_n + lane_p)
            dg[at(layer, r), :] = jnp.where(here > 0, 0.5 * (6.0 * here + around), 0.0)

            def face(other):
                return jnp.where((here > 0) & (other > 0), -0.5 * (here + other), 0.0)

            fx[at(layer, r), :] = face(above)
            fyn[at(layer, r), :] = face(row_n)
            fyp[at(layer, r), :] = face(row_p)
            fzn[at(layer, r), :] = face(lane_n)
            fzp[at(layer, r), :] = face(lane_p)
            below, here = here, above

    repeat(0, steps, 2, prepare)
    full = [jnp.full((SUB, lanes), scal[k], jnp.float32) for k in range(6)]
    wait(False)

    def sweep(ref, first, count, r, emit):
        below = [ref[c, at(first - 1, r), :] for c in range(cols)]
        here = [ref[c, at(first, r), :] for c in range(cols)]
        face_low = fx[at(first - 1, r), :]
        for layer in range(first, first + count):
            above = [ref[c, at(layer + 1, r), :] for c in range(cols)]
            face_high = fx[at(layer, r), :]
            diag = dg[at(layer, r), :]
            row_n, row_p = fyn[at(layer, r), :], fyp[at(layer, r), :]
            lane_n, lane_p = fzn[at(layer, r), :], fzp[at(layer, r), :]
            for c in range(cols):
                v = here[c]
                along_x = face_high * above[c] + face_low * below[c]
                along_y = row_n * ref[c, at(layer, r, 1), :] + row_p * ref[c, at(layer, r, -1), :]
                along_z = lane_n * pltpu.roll(v, lanes - 1, 1) + lane_p * pltpu.roll(v, 1, 1)
                emit(layer, c, v, (diag * v + along_x) + (along_y + along_z))
            below, here, face_low = here, above, face_high

    def store(ref, layer, c, r, value):
        ref[c, at(layer, r), :] = value

    def first_half(i):
        r = i * SUB
        sweep(b, 1, window - 2, r, lambda l, c, v, a: store(y, l, c, r, full[1] * v + full[2] * a))

    def first_end(i):
        r = i * SUB
        sweep(y, 2, window - 4, r, lambda l, c, v, a: store(z, l, c, r, full[0] * b[c, at(l, r), :] + a))

    def second_half(i):
        r = i * SUB
        sweep(z, 3, window - 6, r, lambda l, c, v, a: store(y, l, c, r, full[4] * v + full[5] * a))

    def second_end(i):
        r = i * SUB
        sweep(y, own, own, r, lambda l, c, v, a: store(b, l, c, r, full[3] * z[c, at(l, r), :] + a))

    base = len(spots)
    leaving = []

    def leave(ref, adi, part):
        for layer in range(own):
            spot = (own + layer) * rows + part * part_rows
            copy = pltpu.make_async_copy(
                ref.at[:, pl.ds(spot, part_rows)],
                out.at[layer // per, part, adi, :, layer % per],
                sems.at[base + len(leaving)],
            )
            copy.start()
            leaving.append(copy)

    repeat(0, steps, 2, first_half)
    repeat(0, steps, 2, first_end)
    for part in range(parts):
        leave(z, 0, part)
    repeat(0, steps, 3, second_half)
    for part in range(parts):
        repeat(part * steps // parts, (part + 1) * steps // parts, 3, second_end)
        leave(b, 1, part)
    for copy in leaving:
        copy.wait()


def factors(parts, cols, rows, per, side, scal, table, pieces, after):
    lanes = pieces[0][0].shape[-1]
    layers = 6 * per
    size = layers * rows
    work = cols * size * lanes
    out = (2, parts, ADI, cols, per, rows // parts, lanes)
    spots = [p[1:] for p in pieces]
    flat = pltpu.VMEM((size, lanes), jnp.float32)
    return pl.pallas_call(
        functools.partial(factor_kernel, spots, parts, rows),
        out_shape=jax.ShapeDtypeStruct(out, jnp.float32),
        in_specs=[SCALARS] * 3 + [ANY] * (len(pieces) + len(after)),
        out_specs=ANY,
        scratch_shapes=[pltpu.VMEM((cols, size, lanes), jnp.float32)] * 3
        + [flat] * 7
        + [pltpu.SemaphoreType.DMA((len(pieces) + 2 * ADI * per * parts,))],
        compiler_params=pltpu.CompilerParams(vmem_limit_bytes=VMEM_BYTES),
        cost_estimate=pl.CostEstimate(flops=200000 * work, bytes_accessed=480 * work, transcendentals=0),
        name="factors",
    )(side, scal, table, *(p[0] for p in pieces), *after)


def place_kernel(moved, *refs):
    ctrl, obsv = refs[-2:]
    half = moved.shape[3] // 2
    for spot in range(2):
        for adi in range(ADI):
            ctrl[adi, 0, spot] = moved[spot, 0, adi, :half]
            obsv[adi, 0, spot] = moved[spot, 0, adi, half:]


def place(start, width, half, moved, held):
    _, parts, adi, cols, per, rows, lanes = moved.shape
    block = pl.BlockSpec((2, 1, adi, cols, per, rows, lanes), lambda i: (0, i, 0, 0, 0, 0, 0))
    out_block = pl.BlockSpec(
        (adi, 1, 2, width, per, rows, lanes), lambda i: (0, i, 0, start // width, 0, 0, 0)
    )
    out_shape = jax.ShapeDtypeStruct((adi, parts, 2, half, per, rows, lanes), jnp.float32)
    return pl.pallas_call(
        place_kernel,
        grid=(parts,),
        out_shape=(out_shape, out_shape),
        in_specs=[block] + [ANY] * len(held),
        out_specs=(out_block, out_block),
        input_output_aliases={1 + i: i for i in range(len(held))},
        compiler_params=pltpu.CompilerParams(vmem_limit_bytes=VMEM_BYTES),
        cost_estimate=pl.CostEstimate(flops=0, bytes_accessed=8 * moved.size, transcendentals=0),
        name="place",
    )(moved, *held)


def split16(value):
    high = value.astype(jnp.bfloat16)
    return high, (value - high.astype(jnp.float32)).astype(jnp.bfloat16)


def gram_kernel(ctrl, obsv, out, left, right):
    adi, cols, _, rows, lanes = ctrl.shape
    total = adi * cols

    @pl.when((pl.program_id(0) == 0) & (pl.program_id(1) == 0))
    def _():
        out[...] = jnp.zeros_like(out)

    for a in range(adi):
        left[pl.ds(a * cols * rows, cols * rows), :] = ctrl[a, :, 0].reshape(cols * rows, lanes)
        right[pl.ds(a * cols * rows, cols * rows), :] = obsv[a, :, 0].reshape(cols * rows, lanes)

    def pair(ref, row):
        values = [ref[pl.ds(row + k, total, stride=rows), :] for k in range(2)]
        return split16(jnp.concatenate(values, axis=1))

    def dot(a, b):
        return lax.dot_general(a, b, (((1,), (1,)), ((), ())), preferred_element_type=jnp.float32)

    summed = out[...]
    for row in range(0, rows, 2):
        a_high, a_low = pair(left, row)
        b_high, b_low = pair(right, row)
        summed = summed + (dot(a_high, b_high) + (dot(a_high, b_low) + dot(a_low, b_high)))
    out[...] = summed


def gram(ctrl, obsv):
    adi, cols, per, rows, lanes = ctrl.shape
    chunk = 16
    block = pl.BlockSpec((adi, cols, 1, chunk, lanes), lambda i, j: (0, 0, i, j, 0))
    total = adi * cols
    return pl.pallas_call(
        gram_kernel,
        grid=(per, rows // chunk),
        out_shape=jax.ShapeDtypeStruct((total, total), jnp.float32),
        in_specs=[block, block],
        out_specs=pl.BlockSpec((total, total), lambda i, j: (0, 0)),
        scratch_shapes=[pltpu.VMEM((total * chunk, lanes), jnp.float32)] * 2,
        compiler_params=pltpu.CompilerParams(vmem_limit_bytes=VMEM_BYTES),
        cost_estimate=pl.CostEstimate(
            flops=6 * total * total * per * rows * lanes, bytes_accessed=8 * ctrl.size, transcendentals=0
        ),
        name="gram",
    )(ctrl, obsv)


def body(input_map, output_map, region_ids, region_cond, shift_ids):
    slabs, parts = lax.axis_size("slab"), lax.axis_size("col")
    col_local, per, rows, lanes = input_map.shape
    total_x = per * slabs
    parity = lax.rem(lax.axis_index("slab"), 2)
    side = parity.reshape(1).astype(jnp.int32)
    swap = [(i, i ^ 1) for i in range(slabs)]
    upward = [(i, i + 2) for i in range(slabs - 2)]
    downward = [(i + 2, i) for i in range(slabs - 2)]

    cond_max = jnp.max(region_cond)
    shifts = 0.25 * jnp.exp2(shift_ids.astype(jnp.float32))
    scal = factor_scalars(shifts, cond_max)

    maps = [m.reshape(col_local, per * rows, lanes) for m in (input_map, output_map)]
    ids = region_ids.reshape(per * rows, lanes)
    half = col_local // 2
    unit = half // sum(WIDTHS)
    widths = [unit * w for w in WIDTHS]
    total = len(widths)
    order = sorted(range(total), key=lambda g: (-widths[g], g))
    starts = [sum(widths[h] for h in order[: order.index(g)]) for g in range(total)]
    counts = [2 * w for w in widths]

    def exchange(x):
        return lax.ppermute(x, "slab", swap)

    def kept(group, out, to, first=0):
        w = widths[group]
        return [(first + k, starts[group], half, w, out, to + k * w) for k in range(2)]

    def sent(group, out, to, first=0):
        w = widths[group]
        return [(first + k, half + starts[group], -half, w, out, to + k * w) for k in range(2)]

    got, halos = {}, []

    def halo(message):
        up = down = message
        if halos:
            up, lo = lax.optimization_barrier((message, halos[-1][0]))
            down, hi = lax.optimization_barrier((message, halos[-1][1]))
            halos[-1] = (lo, hi)
        halos.append((lax.ppermute(up, "slab", upward), lax.ppermute(down, "slab", downward)))

    n = counts[0]
    pieces = sent(0, 0, 0) + [(None, 0, 0, 1, 0, n)] + kept(0, 1, 0) + [(None, 0, 0, 1, 1, n)]
    outgoing, message = pack(side, maps, pieces, (n + 1, n + 1), ids=ids)
    got[0] = (exchange(outgoing), 0)
    halo(message)

    m = counts[1]
    pieces = [(0, 0, 0, n, 0, 0), (0, n, 0, 1, 0, n + m)] + kept(1, 0, n, 1) + sent(1, 1, 0, 1)
    message, outgoing = pack(
        side, [got[0][0]] + maps, pieces, (n + m + 1, m), after=halos[0]
    )
    halo(message)
    got[1] = (exchange(outgoing), 0)

    begins = {g: sum(counts[3:g]) for g in range(3, total)}
    pieces = [(0, 0, 0, m, 2, 0)] + kept(2, 2, m, 1) + sent(2, 0, 0, 1)
    for g in range(3, total):
        pieces += sent(g, 1, begins[g], 1)
    outgoing, later, message = pack(
        side, [got[1][0]] + maps, pieces, (counts[2], sum(counts[3:]), m + counts[2])
    )
    halo(message)
    second = exchange(outgoing)
    later, second = lax.optimization_barrier((later, second))
    rest = exchange(later)
    pieces = []
    for g in range(2, total):
        got[g] = (second, 0) if g == 2 else (rest, begins[g])
        pieces.append((int(g > 2), got[g][1], 0, counts[g], g - 2, 0))
        if g + 1 < total:
            pieces += kept(g + 1, g - 2, counts[g], 2)
    lengths = [counts[g] + (counts[g + 1] if g + 1 < total else 0) for g in range(2, total)]
    messages = pack(side, [second, rest] + maps, pieces, lengths)

    region_float = (ids + 1).astype(jnp.float32)[None]
    held = ()
    for group in range(total):
        n = counts[group]
        if 0 < group < total - 1:
            halo(messages[group - 1])
        after = messages if group == 0 else ()
        (lo_kept, hi_kept), (lo_got, hi_got) = halos[group], halos[group + 1]
        before = counts[group - 1] if group else 0
        (lo_a, hi_a), (lo_b, hi_b) = halos[0], halos[1]
        pieces = [
            (lo_a, counts[0], 0, 0, False, 0),
            (hi_a, counts[0], 0, 2, False, 0),
            (lo_b, counts[0] + counts[1], 0, 0, True, 0),
            (hi_b, counts[0] + counts[1], 0, 2, True, 0),
            (region_float, 0, 0, 1, False, 0),
            (got[0][0], counts[0], 0, 1, True, 0),
            (lo_kept, before, n, 0, False, 0),
            (hi_kept, before, n, 2, False, 0),
            (maps[0], (starts[group], half), n // 2, 1, False, 0),
            (maps[1], (starts[group], half), n // 2, 1, False, n // 2),
            (got[group][0], got[group][1], n, 1, True, 0),
            (lo_got, 0, n, 0, True, 0),
            (hi_got, 0, n, 2, True, 0),
        ]
        result = factors(parts, n, rows, per, side, scal, region_cond, pieces, after)
        result = result.reshape(2 * parts, *result.shape[2:])
        pairs = [[k * 2 * parts + j for j in range(2 * parts)] for k in range(slabs // 2)]
        moved = lax.all_to_all(
            result, ("slab", "col"), split_axis=0, concat_axis=0, axis_index_groups=pairs, tiled=True
        )
        moved = moved.reshape(2, parts, *moved.shape[1:])
        held = place(starts[group], widths[group], half, moved, held)

    ctrl, obsv = (x.reshape(ADI, parts * col_local, per, rows // parts, lanes) for x in held)
    partial_value = gram(ctrl, obsv)
    count = partial_value.shape[0]
    tiles = partial_value.reshape(slabs, count // slabs, parts, count // parts).transpose(0, 2, 1, 3)
    tiles = tiles.reshape(slabs * parts, count // slabs, count // parts)
    tiles = lax.all_to_all(tiles, ("slab", "col"), split_axis=0, concat_axis=0, tiled=True)
    norm_scale = 1.0 / math.sqrt(total_x * rows * lanes)
    return (ctrl, obsv, jnp.sum(tiles, 0) * norm_scale)


def solution(mesh):
    placed = (
        P("col", "slab", None, None),
        P("col", "slab", None, None),
        P("slab", None, None),
        P(),
        P(),
    )
    return jax.shard_map(
        body,
        mesh=mesh,
        in_specs=placed,
        out_specs=(
            P(None, None, "slab", "col", None),
            P(None, None, "slab", "col", None),
            P("slab", "col"),
        ),
        check_vma=False,
    )
```

```python
import functools
import math

import jax
import jax.numpy as jnp
from jax import lax
from jax.experimental import pallas as pl
from jax.experimental.pallas import tpu as pltpu
from jax.sharding import PartitionSpec as P

ADI = 2
STEPS = 3
WIDTHS = (1, 2, 2, 2, 1)
SUB = 8
VMEM_BYTES = 50 * 1024 * 1024
ANY = pl.BlockSpec(memory_space=pl.ANY)
IN_VMEM = pl.BlockSpec(memory_space=pltpu.VMEM)
SCALARS = pl.BlockSpec(memory_space=pltpu.SMEM)


def solve_polynomial(shift_val, cond_max):
    high_eig = shift_val + 12.0 * cond_max
    mid_eig = 0.5 * (high_eig + shift_val)
    half_span = 0.5 * (high_eig - shift_val)
    ratio_eig = mid_eig / half_span
    rho_now = 1.0 / ratio_eig
    zero = jnp.zeros_like(mid_eig)
    total = [zero] * STEPS
    residual = [jnp.ones_like(mid_eig)] + [zero] * (STEPS - 1)
    direction = [1.0 / mid_eig] + [zero] * (STEPS - 1)
    for step in range(STEPS):
        total = [t + d for t, d in zip(total, direction)]
        if step < STEPS - 1:
            raised = [zero] + direction[:-1]
            residual = [r - (u + shift_val * d) for r, u, d in zip(residual, raised, direction)]
            rho_next = 1.0 / (2.0 * ratio_eig - rho_now)
            direction = [
                rho_next * rho_now * d + 2.0 * rho_next / half_span * r
                for d, r in zip(direction, residual)
            ]
            rho_now = rho_next
    return total


def factor_scalars(shifts, cond_max):
    first = solve_polynomial(shifts[0], cond_max)
    second = solve_polynomial(shifts[1], cond_max)
    scale_first = jnp.sqrt(2.0 * shifts[0])
    scale_second = jnp.sqrt(2.0 * shifts[1]) / scale_first
    both = shifts[0] + shifts[1]
    rest = [1.0 - both * second[0], -both * second[1], -both * second[2]]
    return jnp.stack([scale_first * c for c in first] + [scale_second * c for c in rest])


def pack(side, sources, pieces, counts, after=(), ids=None):
    size, lanes = sources[0].shape[1:]
    held = len(sources) + len(after) + (ids is not None)

    def kernel(*refs):
        side_ref, operands = refs[0], refs[1 : 1 + held]
        outs = refs[1 + held : 1 + held + len(counts)]
        sems = refs[-1]
        copies = []
        for k, (source, start, step, count, out, to) in enumerate(pieces):
            if source is not None:
                block = operands[source].at[pl.ds(start + step * side_ref[0], count)]
                copy = pltpu.make_async_copy(block, outs[out].at[pl.ds(to, count)], sems.at[k])
                copy.start()
                copies.append(copy)
        for source, _, _, _, out, to in pieces:
            if source is None:
                outs[out][to] = (operands[held - 1][...] + 1).astype(jnp.float32)
        for copy in copies:
            copy.wait()

    extra, specs = ([ids], [IN_VMEM]) if ids is not None else ([], [])
    moved = 4 * sum(p[3] for p in pieces) * size * lanes
    return pl.pallas_call(
        kernel,
        out_shape=[jax.ShapeDtypeStruct((c, size, lanes), jnp.float32) for c in counts],
        in_specs=[SCALARS] + [ANY] * (len(sources) + len(after)) + specs,
        out_specs=[IN_VMEM] * len(counts),
        scratch_shapes=[pltpu.SemaphoreType.DMA((len(pieces),))],
        compiler_params=pltpu.CompilerParams(vmem_limit_bytes=VMEM_BYTES),
        cost_estimate=pl.CostEstimate(flops=0, bytes_accessed=2 * moved, transcendentals=0),
        name="pack",
    )(side, *sources, *after, *extra)


def factor_kernel(spots, parts, rows, side, scal, table, *refs):
    data, (b, y, z, cond, dg, fx, fyn, fyp, fzn, fzp, sems) = refs[: len(spots)], refs[-11:]
    outs = refs[-11 - 2 * parts : -11]
    cols, size, lanes = b.shape
    window = size // rows
    per = window // 6
    own = 2 * per
    slab = per * rows
    part_rows = rows // parts
    steps = rows // SUB
    parity, mine = side[0], side[1]

    copies = []
    for k, (start, count, block, other, to) in enumerate(spots):
        spot = 1 - parity if other else parity
        at = pl.ds(pl.multiple_of((block * 2 + spot) * slab, SUB), slab)
        if count == 0:
            copy = pltpu.make_async_copy(data[k].at[start], fx.at[at], sems.at[k])
        else:
            place_at = b.at[pl.ds(to, count), at]
            if isinstance(start, tuple):
                start = start[0] + start[1] * parity
            copy = pltpu.make_async_copy(data[k].at[pl.ds(start, count)], place_at, sems.at[k])
        copy.start()
        copies.append(copy)

    def wait(ids):
        for (_, count, *_), copy in zip(spots, copies):
            if (count == 0) == ids:
                copy.wait()

    def at(layer, r, shift=0):
        spot = layer * rows + r
        return pl.ds(spot + shift if shift else pl.multiple_of(spot, SUB), SUB)

    def repeat(first, count, times, body):
        while count % times:
            times -= 1

        def turn(i, carry):
            for k in range(times):
                body(first + i * times + k)
            return carry

        lax.fori_loop(0, count // times, turn, 0)

    wait(True)
    levels = [table[k] for k in range(table.shape[0])]

    def fill(i):
        r = i * SUB
        for layer in range(window):
            index = fx[at(layer, r), :]
            value = jnp.zeros_like(index)
            for k, level in enumerate(levels):
                value = jnp.where(index == float(k + 1), level, value)
            cond[at(layer, r), :] = value

    repeat(0, steps, 4, fill)
    row = lax.broadcasted_iota(jnp.int32, (SUB, lanes), 0)
    lane = lax.broadcasted_iota(jnp.int32, (SUB, lanes), 1)

    def prepare(i):
        r = i * SUB
        below, here = cond[at(0, r), :], cond[at(1, r), :]
        fx[at(0, r), :] = jnp.where((below > 0) & (here > 0), -0.5 * (below + here), 0.0)
        for layer in range(1, window - 1):
            above = cond[at(layer + 1, r), :]
            row_n = jnp.where(row + r < rows - 1, cond[at(layer, r, 1), :], 0.0)
            row_p = jnp.where(row + r > 0, cond[at(layer, r, -1), :], 0.0)
            lane_n = jnp.where(lane < lanes - 1, pltpu.roll(here, lanes - 1, 1), 0.0)
            lane_p = jnp.where(lane > 0, pltpu.roll(here, 1, 1), 0.0)
            around = (above + below) + (row_n + row_p) + (lane_n + lane_p)
            dg[at(layer, r), :] = jnp.where(here > 0, 0.5 * (6.0 * here + around), 0.0)

            def face(other):
                return jnp.where((here > 0) & (other > 0), -0.5 * (here + other), 0.0)

            fx[at(layer, r), :] = face(above)
            fyn[at(layer, r), :] = face(row_n)
            fyp[at(layer, r), :] = face(row_p)
            fzn[at(layer, r), :] = face(lane_n)
            fzp[at(layer, r), :] = face(lane_p)
            below, here = here, above

    repeat(0, steps, 2, prepare)
    full = [jnp.full((SUB, lanes), scal[k], jnp.float32) for k in range(6)]
    wait(False)

    def sweep(ref, first, count, r, emit):
        below = [ref[c, at(first - 1, r), :] for c in range(cols)]
        here = [ref[c, at(first, r), :] for c in range(cols)]
        face_low = fx[at(first - 1, r), :]
        for layer in range(first, first + count):
            above = [ref[c, at(layer + 1, r), :] for c in range(cols)]
            face_high = fx[at(layer, r), :]
            diag = dg[at(layer, r), :]
            row_n, row_p = fyn[at(layer, r), :], fyp[at(layer, r), :]
            lane_n, lane_p = fzn[at(layer, r), :], fzp[at(layer, r), :]
            for c in range(cols):
                v = here[c]
                along_x = face_high * above[c] + face_low * below[c]
                along_y = row_n * ref[c, at(layer, r, 1), :] + row_p * ref[c, at(layer, r, -1), :]
                along_z = lane_n * pltpu.roll(v, lanes - 1, 1) + lane_p * pltpu.roll(v, 1, 1)
                emit(layer, c, v, (diag * v + along_x) + (along_y + along_z))
            below, here, face_low = here, above, face_high

    def store(ref, layer, c, r, value):
        ref[c, at(layer, r), :] = value

    def first_half(i):
        r = i * SUB
        sweep(b, 1, window - 2, r, lambda l, c, v, a: store(y, l, c, r, full[1] * v + full[2] * a))

    def first_end(i):
        r = i * SUB
        sweep(y, 2, window - 4, r, lambda l, c, v, a: store(z, l, c, r, full[0] * b[c, at(l, r), :] + a))

    def second_half(i):
        r = i * SUB
        sweep(z, 3, window - 6, r, lambda l, c, v, a: store(y, l, c, r, full[4] * v + full[5] * a))

    def second_end(i):
        r = i * SUB
        sweep(y, own, own, r, lambda l, c, v, a: store(b, l, c, r, full[3] * z[c, at(l, r), :] + a))

    base = len(spots)
    leaving = []

    def leave(ref, adi, hop):
        part = lax.bitwise_xor(mine, hop)
        for other in range(2):
            first = own + (1 - parity if other else parity) * per
            for layer in range(per):
                spot = pl.multiple_of((first + layer) * rows + part * part_rows, SUB)
                copy = pltpu.make_async_copy(
                    ref.at[:, pl.ds(spot, part_rows)],
                    outs[other * parts + hop].at[adi, :, layer],
                    sems.at[base + len(leaving)],
                )
                copy.start()
                leaving.append(copy)

    repeat(0, steps, 2, first_half)
    repeat(0, steps, 2, first_end)
    for hop in range(parts):
        leave(z, 0, hop)
    repeat(0, steps, 3, second_half)
    for hop in reversed(range(parts)):
        repeat(lax.bitwise_xor(mine, hop) * (steps // parts), steps // parts, 3, second_end)
        leave(b, 1, hop)
    for copy in leaving:
        copy.wait()


def factors(parts, cols, rows, per, side, scal, table, pieces, after):
    lanes = pieces[0][0].shape[-1]
    layers = 6 * per
    size = layers * rows
    work = cols * size * lanes
    out = jax.ShapeDtypeStruct((ADI, cols, per, rows // parts, lanes), jnp.float32)
    spots = [p[1:] for p in pieces]
    flat = pltpu.VMEM((size, lanes), jnp.float32)
    return pl.pallas_call(
        functools.partial(factor_kernel, spots, parts, rows),
        out_shape=[out] * (2 * parts),
        in_specs=[SCALARS] * 3 + [ANY] * (len(pieces) + len(after)),
        out_specs=[ANY] * (2 * parts),
        scratch_shapes=[pltpu.VMEM((cols, size, lanes), jnp.float32)] * 3
        + [flat] * 7
        + [pltpu.SemaphoreType.DMA((len(pieces) + 2 * ADI * per * parts,))],
        compiler_params=pltpu.CompilerParams(vmem_limit_bytes=VMEM_BYTES),
        cost_estimate=pl.CostEstimate(flops=200000 * work, bytes_accessed=480 * work, transcendentals=0),
        name="factors",
    )(side, scal, table, *(p[0] for p in pieces), *after)


def place_kernel(start, width, parts, side, *refs):
    moved, (ctrl, obsv, token, held, sems) = refs[: 2 * parts], refs[-5:]
    entering = []
    for k, block in enumerate(moved):
        copy = pltpu.make_async_copy(block, held.at[k], sems.at[k])
        copy.start()
        entering.append(copy)
    token[...] = jnp.zeros_like(token)
    leaving = []
    for k, copy in enumerate(entering):
        copy.wait()
        half, part = lax.bitwise_xor(side[0], k // parts), lax.bitwise_xor(side[1], k % parts)
        for adi in range(ADI):
            for first, out in ((0, ctrl), (width, obsv)):
                copy = pltpu.make_async_copy(
                    held.at[k, adi, pl.ds(first, width)],
                    out.at[adi, part, half, pl.ds(start, width)],
                    sems.at[2 * parts + len(leaving)],
                )
                copy.start()
                leaving.append(copy)
    for copy in leaving:
        copy.wait()


def place(side, parts, start, width, half, moved, held):
    adi, cols, per, rows, lanes = moved[0].shape
    out_shape = jax.ShapeDtypeStruct((adi, parts, 2, half, per, rows, lanes), jnp.float32)
    token = jax.ShapeDtypeStruct((8, 128), jnp.float32)
    count = len(moved)
    return pl.pallas_call(
        functools.partial(place_kernel, start, width, parts),
        out_shape=(out_shape, out_shape, token),
        in_specs=[SCALARS] + [ANY] * (count + len(held)),
        out_specs=(ANY, ANY, IN_VMEM),
        input_output_aliases={1 + count + i: i for i in range(len(held))},
        scratch_shapes=[
            pltpu.VMEM((count, *moved[0].shape), jnp.float32),
            pltpu.SemaphoreType.DMA((count * (1 + 2 * adi),)),
        ],
        compiler_params=pltpu.CompilerParams(vmem_limit_bytes=VMEM_BYTES),
        cost_estimate=pl.CostEstimate(
            flops=0, bytes_accessed=8 * count * moved[0].size, transcendentals=0
        ),
        name="place",
    )(side, *moved, *held)


def split16(value):
    high = value.astype(jnp.bfloat16)
    return high, (value - high.astype(jnp.float32)).astype(jnp.bfloat16)


def gram_kernel(ctrl, obsv, out, left, right):
    adi, cols, _, rows, lanes = ctrl.shape
    total = adi * cols

    @pl.when((pl.program_id(0) == 0) & (pl.program_id(1) == 0))
    def _():
        out[...] = jnp.zeros_like(out)

    for a in range(adi):
        left[pl.ds(a * cols * rows, cols * rows), :] = ctrl[a, :, 0].reshape(cols * rows, lanes)
        right[pl.ds(a * cols * rows, cols * rows), :] = obsv[a, :, 0].reshape(cols * rows, lanes)

    def pair(ref, row):
        values = [ref[pl.ds(row + k, total, stride=rows), :] for k in range(2)]
        return split16(jnp.concatenate(values, axis=1))

    def dot(a, b):
        return lax.dot_general(a, b, (((1,), (1,)), ((), ())), preferred_element_type=jnp.float32)

    summed = out[...]
    for row in range(0, rows, 2):
        a_high, a_low = pair(left, row)
        b_high, b_low = pair(right, row)
        summed = summed + (dot(a_high, b_high) + (dot(a_high, b_low) + dot(a_low, b_high)))
    out[...] = summed


def gram(ctrl, obsv):
    adi, cols, per, rows, lanes = ctrl.shape
    chunk = 16
    block = pl.BlockSpec((adi, cols, 1, chunk, lanes), lambda i, j: (0, 0, i, j, 0))
    total = adi * cols
    return pl.pallas_call(
        gram_kernel,
        grid=(per, rows // chunk),
        out_shape=jax.ShapeDtypeStruct((total, total), jnp.float32),
        in_specs=[block, block],
        out_specs=pl.BlockSpec((total, total), lambda i, j: (0, 0)),
        scratch_shapes=[pltpu.VMEM((total * chunk, lanes), jnp.float32)] * 2,
        compiler_params=pltpu.CompilerParams(vmem_limit_bytes=VMEM_BYTES),
        cost_estimate=pl.CostEstimate(
            flops=6 * total * total * per * rows * lanes, bytes_accessed=8 * ctrl.size, transcendentals=0
        ),
        name="gram",
    )(ctrl, obsv)


def body(input_map, output_map, region_ids, region_cond, shift_ids):
    slabs, parts = lax.axis_size("slab"), lax.axis_size("col")
    col_local, per, rows, lanes = input_map.shape
    total_x = per * slabs
    parity = lax.rem(lax.axis_index("slab"), 2)
    side = jnp.stack([parity, lax.axis_index("col")]).astype(jnp.int32)
    swap = [(i, i ^ 1) for i in range(slabs)]
    upward = [(i, i + 2) for i in range(slabs - 2)]
    downward = [(i + 2, i) for i in range(slabs - 2)]

    cond_max = jnp.max(region_cond)
    shifts = 0.25 * jnp.exp2(shift_ids.astype(jnp.float32))
    scal = factor_scalars(shifts, cond_max)

    maps = [m.reshape(col_local, per * rows, lanes) for m in (input_map, output_map)]
    ids = region_ids.reshape(per * rows, lanes)
    half = col_local // 2
    unit = half // sum(WIDTHS)
    widths = [unit * w for w in WIDTHS]
    total = len(widths)
    order = sorted(range(total), key=lambda g: (-widths[g], g))
    starts = [sum(widths[h] for h in order[: order.index(g)]) for g in range(total)]
    counts = [2 * w for w in widths]

    def exchange(x):
        return lax.ppermute(x, "slab", swap)

    def kept(group, out, to, first=0):
        w = widths[group]
        return [(first + k, starts[group], half, w, out, to + k * w) for k in range(2)]

    def sent(group, out, to, first=0):
        w = widths[group]
        return [(first + k, half + starts[group], -half, w, out, to + k * w) for k in range(2)]

    got, halos = {}, []

    def halo(message):
        up = down = message
        if halos:
            up, lo = lax.optimization_barrier((message, halos[-1][0]))
            down, hi = lax.optimization_barrier((message, halos[-1][1]))
            halos[-1] = (lo, hi)
        halos.append((lax.ppermute(up, "slab", upward), lax.ppermute(down, "slab", downward)))

    n, m = counts[:2]
    pieces = sent(0, 0, 0) + sent(1, 0, n) + [(None, 0, 0, 1, 0, n + m)]
    pieces += kept(0, 1, 0) + [(None, 0, 0, 1, 1, n)]
    outgoing, message = pack(side, maps, pieces, (n + m + 1, n + 1), ids=ids)
    early = exchange(outgoing)
    halo(message)
    got[0], got[1] = (early, 0), (early, n)

    pieces = [(0, 0, 0, n, 0, 0), (0, n + m, 0, 1, 0, n + m)] + kept(1, 0, n, 1)
    pieces += [(0, n, 0, m, 1, 0)] + kept(2, 1, m, 1)
    begins = {g: sum(counts[2:g]) for g in range(2, total)}
    for g in range(2, total):
        pieces += sent(g, 2, begins[g], 1)
    message, following, outgoing = pack(
        side,
        [early] + maps,
        pieces,
        (n + m + 1, m + counts[2], sum(counts[2:])),
        after=halos[0],
    )
    halo(message)
    later = exchange(outgoing)
    halo(following)
    pieces = []
    for g in range(2, total):
        got[g] = (later, begins[g])
        pieces.append((0, begins[g], 0, counts[g], g - 2, 0))
        if g + 1 < total:
            pieces += kept(g + 1, g - 2, counts[g], 1)
    lengths = [counts[g] + (counts[g + 1] if g + 1 < total else 0) for g in range(2, total)]
    messages = pack(side, [later] + maps, pieces, lengths)

    region_float = (ids + 1).astype(jnp.float32)[None]
    held, tokens = (), []
    for group in range(total):
        n = counts[group]
        if 0 < group < total - 1:
            halo(messages[group - 1])
        after = tuple(messages) if group == 0 else tuple(tokens[group - 2 : group - 1])
        (lo_kept, hi_kept), (lo_got, hi_got) = halos[group], halos[group + 1]
        before = counts[group - 1] if group else 0
        (lo_a, hi_a), (lo_b, hi_b) = halos[0], halos[1]
        pieces = [
            (lo_a, counts[0], 0, 0, False, 0),
            (hi_a, counts[0], 0, 2, False, 0),
            (lo_b, counts[0] + counts[1], 0, 0, True, 0),
            (hi_b, counts[0] + counts[1], 0, 2, True, 0),
            (region_float, 0, 0, 1, False, 0),
            (early, counts[0] + counts[1], 0, 1, True, 0),
            (lo_kept, before, n, 0, False, 0),
            (hi_kept, before, n, 2, False, 0),
            (maps[0], (starts[group], half), n // 2, 1, False, 0),
            (maps[1], (starts[group], half), n // 2, 1, False, n // 2),
            (got[group][0], got[group][1], n, 1, True, 0),
            (lo_got, 0, n, 0, True, 0),
            (hi_got, 0, n, 2, True, 0),
        ]
        result = factors(parts, n, rows, per, side, scal, region_cond, pieces, after)
        moved = list(result)
        for k in [*range(parts, 2 * parts), *range(1, parts)]:
            pairs = [
                (i * parts + j, (i ^ (k // parts)) * parts + (j ^ (k % parts)))
                for i in range(slabs)
                for j in range(parts)
            ]
            moved[k] = lax.ppermute(result[k], ("slab", "col"), pairs)
        *held, token = place(side, parts, starts[group], widths[group], half, moved, held)
        tokens.append(token)

    ctrl, obsv = (x.reshape(ADI, parts * col_local, per, rows // parts, lanes) for x in held)
    partial_value = gram(ctrl, obsv)
    count = partial_value.shape[0]
    tiles = partial_value.reshape(slabs, count // slabs, parts, count // parts).transpose(0, 2, 1, 3)
    tiles = tiles.reshape(slabs * parts, count // slabs, count // parts)
    tiles = lax.all_to_all(tiles, ("slab", "col"), split_axis=0, concat_axis=0, tiled=True)
    norm_scale = 1.0 / math.sqrt(total_x * rows * lanes)
    return (ctrl, obsv, jnp.sum(tiles, 0) * norm_scale)


def solution(mesh):
    placed = (
        P("col", "slab", None, None),
        P("col", "slab", None, None),
        P("slab", None, None),
        P(),
        P(),
    )
    return jax.shard_map(
        body,
        mesh=mesh,
        in_specs=placed,
        out_specs=(
            P(None, None, "slab", "col", None),
            P(None, None, "slab", "col", None),
            P("slab", "col"),
        ),
        check_vma=False,
    )
```

```python
import functools
import math

import jax
import jax.numpy as jnp
from jax import lax
from jax.experimental import pallas as pl
from jax.experimental.pallas import tpu as pltpu
from jax.sharding import PartitionSpec as P

ADI = 2
STEPS = 3
GROUPS = 4
SUB = 8
VMEM_BYTES = 50 * 1024 * 1024
ANY = pl.BlockSpec(memory_space=pl.ANY)
IN_VMEM = pl.BlockSpec(memory_space=pltpu.VMEM)
SCALARS = pl.BlockSpec(memory_space=pltpu.SMEM)


def solve_polynomial(shift_val, cond_max):
    high_eig = shift_val + 12.0 * cond_max
    mid_eig = 0.5 * (high_eig + shift_val)
    half_span = 0.5 * (high_eig - shift_val)
    ratio_eig = mid_eig / half_span
    rho_now = 1.0 / ratio_eig
    zero = jnp.zeros_like(mid_eig)
    total = [zero] * STEPS
    residual = [jnp.ones_like(mid_eig)] + [zero] * (STEPS - 1)
    direction = [1.0 / mid_eig] + [zero] * (STEPS - 1)
    for step in range(STEPS):
        total = [t + d for t, d in zip(total, direction)]
        if step < STEPS - 1:
            raised = [zero] + direction[:-1]
            residual = [r - (u + shift_val * d) for r, u, d in zip(residual, raised, direction)]
            rho_next = 1.0 / (2.0 * ratio_eig - rho_now)
            direction = [
                rho_next * rho_now * d + 2.0 * rho_next / half_span * r
                for d, r in zip(direction, residual)
            ]
            rho_now = rho_next
    return total


def factor_scalars(shifts, cond_max):
    first = solve_polynomial(shifts[0], cond_max)
    second = solve_polynomial(shifts[1], cond_max)
    scale_first = jnp.sqrt(2.0 * shifts[0])
    scale_second = jnp.sqrt(2.0 * shifts[1]) / scale_first
    both = shifts[0] + shifts[1]
    rest = [1.0 - both * second[0], -both * second[1], -both * second[2]]
    return jnp.stack([scale_first * c for c in first] + [scale_second * c for c in rest])


def pack(side, sources, pieces, counts, after=(), ids=None):
    size, lanes = sources[0].shape[1:]
    held = len(sources) + len(after) + (ids is not None)

    def kernel(*refs):
        side_ref, operands = refs[0], refs[1 : 1 + held]
        outs = refs[1 + held : 1 + held + len(counts)]
        sems = refs[-1]
        copies = []
        for k, (source, start, step, count, out, to) in enumerate(pieces):
            if source is not None:
                block = operands[source].at[pl.ds(start + step * side_ref[0], count)]
                copy = pltpu.make_async_copy(block, outs[out].at[pl.ds(to, count)], sems.at[k])
                copy.start()
                copies.append(copy)
        for source, _, _, _, out, to in pieces:
            if source is None:
                outs[out][to] = (operands[held - 1][...] + 1).astype(jnp.float32)
        for copy in copies:
            copy.wait()

    extra, specs = ([ids], [IN_VMEM]) if ids is not None else ([], [])
    moved = 4 * sum(p[3] for p in pieces) * size * lanes
    return pl.pallas_call(
        kernel,
        out_shape=[jax.ShapeDtypeStruct((c, size, lanes), jnp.float32) for c in counts],
        in_specs=[SCALARS] + [ANY] * (len(sources) + len(after)) + specs,
        out_specs=[IN_VMEM] * len(counts),
        scratch_shapes=[pltpu.SemaphoreType.DMA((len(pieces),))],
        compiler_params=pltpu.CompilerParams(vmem_limit_bytes=VMEM_BYTES),
        cost_estimate=pl.CostEstimate(flops=0, bytes_accessed=2 * moved, transcendentals=0),
        name="pack",
    )(side, *sources, *after, *extra)


def factor_kernel(spots, parts, rows, direct, side, scal, table, *refs):
    data, (b, y, z, cond, dg, fx, fyn, fyp, fzn, fzp, sems) = refs[: len(spots)], refs[-11:]
    outs = refs[-11 - 2 * parts : -11] if direct else [refs[-12].at[k] for k in range(2 * parts)]
    cols, size, lanes = b.shape
    window = size // rows
    per = window // 6
    own = 2 * per
    slab = per * rows
    part_rows = rows // parts
    steps = rows // SUB
    parity, mine = side[0], side[1]

    copies = []
    for k, (start, count, block, other, to) in enumerate(spots):
        spot = 1 - parity if other else parity
        at = pl.ds(pl.multiple_of((block * 2 + spot) * slab, SUB), slab)
        if count == 0:
            copy = pltpu.make_async_copy(data[k].at[start], fx.at[at], sems.at[k])
        else:
            place_at = b.at[pl.ds(to, count), at]
            if isinstance(start, tuple):
                start = start[0] + start[1] * parity
            copy = pltpu.make_async_copy(data[k].at[pl.ds(start, count)], place_at, sems.at[k])
        copy.start()
        copies.append(copy)

    def wait(ids):
        for (_, count, *_), copy in zip(spots, copies):
            if (count == 0) == ids:
                copy.wait()

    def at(layer, r, shift=0):
        spot = layer * rows + r
        return pl.ds(spot + shift if shift else pl.multiple_of(spot, SUB), SUB)

    def repeat(first, count, times, body):
        while count % times:
            times -= 1

        def turn(i, carry):
            for k in range(times):
                body(first + i * times + k)
            return carry

        lax.fori_loop(0, count // times, turn, 0)

    wait(True)
    levels = [table[k] for k in range(table.shape[0])]

    def fill(i):
        r = i * SUB
        for layer in range(window):
            index = fx[at(layer, r), :]
            value = jnp.zeros_like(index)
            for k, level in enumerate(levels):
                value = jnp.where(index == float(k + 1), level, value)
            cond[at(layer, r), :] = value

    repeat(0, steps, 4, fill)
    row = lax.broadcasted_iota(jnp.int32, (SUB, lanes), 0)
    lane = lax.broadcasted_iota(jnp.int32, (SUB, lanes), 1)

    def prepare(i):
        r = i * SUB
        below, here = cond[at(0, r), :], cond[at(1, r), :]
        fx[at(0, r), :] = jnp.where((below > 0) & (here > 0), -0.5 * (below + here), 0.0)
        for layer in range(1, window - 1):
            above = cond[at(layer + 1, r), :]
            row_n = jnp.where(row + r < rows - 1, cond[at(layer, r, 1), :], 0.0)
            row_p = jnp.where(row + r > 0, cond[at(layer, r, -1), :], 0.0)
            lane_n = jnp.where(lane < lanes - 1, pltpu.roll(here, lanes - 1, 1), 0.0)
            lane_p = jnp.where(lane > 0, pltpu.roll(here, 1, 1), 0.0)
            around = (above + below) + (row_n + row_p) + (lane_n + lane_p)
            dg[at(layer, r), :] = jnp.where(here > 0, 0.5 * (6.0 * here + around), 0.0)

            def face(other):
                return jnp.where((here > 0) & (other > 0), -0.5 * (here + other), 0.0)

            fx[at(layer, r), :] = face(above)
            fyn[at(layer, r), :] = face(row_n)
            fyp[at(layer, r), :] = face(row_p)
            fzn[at(layer, r), :] = face(lane_n)
            fzp[at(layer, r), :] = face(lane_p)
            below, here = here, above

    repeat(0, steps, 2, prepare)
    full = [jnp.full((SUB, lanes), scal[k], jnp.float32) for k in range(6)]
    wait(False)

    def sweep(ref, first, count, r, emit):
        below = [ref[c, at(first - 1, r), :] for c in range(cols)]
        here = [ref[c, at(first, r), :] for c in range(cols)]
        face_low = fx[at(first - 1, r), :]
        for layer in range(first, first + count):
            above = [ref[c, at(layer + 1, r), :] for c in range(cols)]
            face_high = fx[at(layer, r), :]
            diag = dg[at(layer, r), :]
            row_n, row_p = fyn[at(layer, r), :], fyp[at(layer, r), :]
            lane_n, lane_p = fzn[at(layer, r), :], fzp[at(layer, r), :]
            for c in range(cols):
                v = here[c]
                along_x = face_high * above[c] + face_low * below[c]
                along_y = row_n * ref[c, at(layer, r, 1), :] + row_p * ref[c, at(layer, r, -1), :]
                along_z = lane_n * pltpu.roll(v, lanes - 1, 1) + lane_p * pltpu.roll(v, 1, 1)
                emit(layer, c, v, (diag * v + along_x) + (along_y + along_z))
            below, here, face_low = here, above, face_high

    def store(ref, layer, c, r, value):
        ref[c, at(layer, r), :] = value

    def first_half(i):
        r = i * SUB
        sweep(b, 1, window - 2, r, lambda l, c, v, a: store(y, l, c, r, full[1] * v + full[2] * a))

    def first_end(i):
        r = i * SUB
        sweep(y, 2, window - 4, r, lambda l, c, v, a: store(z, l, c, r, full[0] * b[c, at(l, r), :] + a))

    def second_half(i):
        r = i * SUB
        sweep(z, 3, window - 6, r, lambda l, c, v, a: store(y, l, c, r, full[4] * v + full[5] * a))

    def second_end(i):
        r = i * SUB
        sweep(y, own, own, r, lambda l, c, v, a: store(b, l, c, r, full[3] * z[c, at(l, r), :] + a))

    base = len(spots)
    leaving = []

    def part_of(k):
        return lax.bitwise_xor(mine, k) if direct else k

    def leave(ref, adi, k):
        part = part_of(k)
        for other in range(2):
            half = (1 - parity if other else parity) if direct else other
            for layer in range(per):
                spot = pl.multiple_of((own + half * per + layer) * rows + part * part_rows, SUB)
                copy = pltpu.make_async_copy(
                    ref.at[:, pl.ds(spot, part_rows)],
                    outs[other * parts + k].at[adi, :, layer],
                    sems.at[base + len(leaving)],
                )
                copy.start()
                leaving.append(copy)

    repeat(0, steps, 2, first_half)
    repeat(0, steps, 2, first_end)
    for k in range(parts):
        leave(z, 0, k)
    repeat(0, steps, 3, second_half)
    for k in reversed(range(parts)):
        repeat(part_of(k) * (steps // parts), steps // parts, 3, second_end)
        leave(b, 1, k)
    for copy in leaving:
        copy.wait()


def factors(parts, cols, rows, per, direct, side, scal, table, pieces, after):
    lanes = pieces[0][0].shape[-1]
    layers = 6 * per
    size = layers * rows
    work = cols * size * lanes
    block = (ADI, cols, per, rows // parts, lanes)
    count = 2 * parts if direct else 1
    out = jax.ShapeDtypeStruct(block if direct else (2 * parts, *block), jnp.float32)
    spots = [p[1:] for p in pieces]
    flat = pltpu.VMEM((size, lanes), jnp.float32)
    return pl.pallas_call(
        functools.partial(factor_kernel, spots, parts, rows, direct),
        out_shape=[out] * count,
        in_specs=[SCALARS] * 3 + [ANY] * (len(pieces) + len(after)),
        out_specs=[ANY] * count,
        scratch_shapes=[pltpu.VMEM((cols, size, lanes), jnp.float32)] * 3
        + [flat] * 7
        + [pltpu.SemaphoreType.DMA((len(pieces) + 2 * ADI * per * parts,))],
        compiler_params=pltpu.CompilerParams(vmem_limit_bytes=VMEM_BYTES),
        cost_estimate=pl.CostEstimate(flops=200000 * work, bytes_accessed=480 * work, transcendentals=0),
        name="factors",
    )(side, scal, table, *(p[0] for p in pieces), *after)


def place_kernel(start, width, parts, direct, side, *refs):
    ctrl, obsv, held, sems = refs[-4:]
    moved = refs[: 2 * parts] if direct else [refs[0].at[k] for k in range(2 * parts)]
    entering = []
    for k, block in enumerate(moved):
        copy = pltpu.make_async_copy(block, held.at[k], sems.at[k])
        copy.start()
        entering.append(copy)
    leaving = []
    for k, copy in enumerate(entering):
        copy.wait()
        half, part = k // parts, k % parts
        if direct:
            half, part = lax.bitwise_xor(side[0], half), lax.bitwise_xor(side[1], part)
        for adi in range(ADI):
            for first, out in ((0, ctrl), (width, obsv)):
                copy = pltpu.make_async_copy(
                    held.at[k, adi, pl.ds(first, width)],
                    out.at[adi, part, half, pl.ds(start, width)],
                    sems.at[2 * parts + len(leaving)],
                )
                copy.start()
                leaving.append(copy)
    for copy in leaving:
        copy.wait()


def place(side, parts, start, width, half, moved, held):
    direct = len(moved) > 1
    adi, cols, per, rows, lanes = block = moved[0].shape[-5:]
    out_shape = jax.ShapeDtypeStruct((adi, parts, 2, half, per, rows, lanes), jnp.float32)
    count = 2 * parts
    return pl.pallas_call(
        functools.partial(place_kernel, start, width, parts, direct),
        out_shape=(out_shape, out_shape),
        in_specs=[SCALARS] + [ANY] * (len(moved) + len(held)),
        out_specs=(ANY, ANY),
        input_output_aliases={1 + len(moved) + i: i for i in range(len(held))},
        scratch_shapes=[
            pltpu.VMEM((count, *block), jnp.float32),
            pltpu.SemaphoreType.DMA((count * (1 + 2 * adi),)),
        ],
        compiler_params=pltpu.CompilerParams(vmem_limit_bytes=VMEM_BYTES),
        cost_estimate=pl.CostEstimate(
            flops=0, bytes_accessed=8 * count * math.prod(block), transcendentals=0
        ),
        name="place",
    )(side, *moved, *held)


def split16(value):
    high = value.astype(jnp.bfloat16)
    return high, (value - high.astype(jnp.float32)).astype(jnp.bfloat16)


def gram_kernel(ctrl, obsv, out, left, right):
    adi, cols, _, rows, lanes = ctrl.shape
    total = adi * cols

    @pl.when((pl.program_id(0) == 0) & (pl.program_id(1) == 0))
    def _():
        out[...] = jnp.zeros_like(out)

    for a in range(adi):
        left[pl.ds(a * cols * rows, cols * rows), :] = ctrl[a, :, 0].reshape(cols * rows, lanes)
        right[pl.ds(a * cols * rows, cols * rows), :] = obsv[a, :, 0].reshape(cols * rows, lanes)

    def pair(ref, row):
        values = [ref[pl.ds(row + k, total, stride=rows), :] for k in range(2)]
        return split16(jnp.concatenate(values, axis=1))

    def dot(a, b):
        return lax.dot_general(a, b, (((1,), (1,)), ((), ())), preferred_element_type=jnp.float32)

    summed = out[...]
    for row in range(0, rows, 2):
        a_high, a_low = pair(left, row)
        b_high, b_low = pair(right, row)
        summed = summed + (dot(a_high, b_high) + (dot(a_high, b_low) + dot(a_low, b_high)))
    out[...] = summed


def gram(ctrl, obsv):
    adi, cols, per, rows, lanes = ctrl.shape
    chunk = 16
    block = pl.BlockSpec((adi, cols, 1, chunk, lanes), lambda i, j: (0, 0, i, j, 0))
    total = adi * cols
    return pl.pallas_call(
        gram_kernel,
        grid=(per, rows // chunk),
        out_shape=jax.ShapeDtypeStruct((total, total), jnp.float32),
        in_specs=[block, block],
        out_specs=pl.BlockSpec((total, total), lambda i, j: (0, 0)),
        scratch_shapes=[pltpu.VMEM((total * chunk, lanes), jnp.float32)] * 2,
        compiler_params=pltpu.CompilerParams(vmem_limit_bytes=VMEM_BYTES),
        cost_estimate=pl.CostEstimate(
            flops=6 * total * total * per * rows * lanes, bytes_accessed=8 * ctrl.size, transcendentals=0
        ),
        name="gram",
    )(ctrl, obsv)


def body(input_map, output_map, region_ids, region_cond, shift_ids):
    slabs, parts = lax.axis_size("slab"), lax.axis_size("col")
    col_local, per, rows, lanes = input_map.shape
    total_x = per * slabs
    parity = lax.rem(lax.axis_index("slab"), 2)
    side = jnp.stack([parity, lax.axis_index("col")]).astype(jnp.int32)
    swap = [(i, i ^ 1) for i in range(slabs)]
    upward = [(i, i + 2) for i in range(slabs - 2)]
    downward = [(i + 2, i) for i in range(slabs - 2)]

    cond_max = jnp.max(region_cond)
    shifts = 0.25 * jnp.exp2(shift_ids.astype(jnp.float32))
    scal = factor_scalars(shifts, cond_max)

    maps = [m.reshape(col_local, per * rows, lanes) for m in (input_map, output_map)]
    ids = region_ids.reshape(per * rows, lanes)
    half = col_local // 2
    width = half // GROUPS
    n = 2 * width

    def exchange(x):
        return lax.ppermute(x, "slab", swap)

    def kept(group, out, to, first=0):
        return [(first + k, group * width, half, width, out, to + k * width) for k in range(2)]

    def sent(group, out, to, first=0):
        return [(first + k, half + group * width, -half, width, out, to + k * width) for k in range(2)]

    got, halos = {}, []

    def halo(message):
        up = down = message
        if halos:
            up, lo = lax.optimization_barrier((message, halos[-1][0]))
            down, hi = lax.optimization_barrier((message, halos[-1][1]))
            halos[-1] = (lo, hi)
        halos.append((lax.ppermute(up, "slab", upward), lax.ppermute(down, "slab", downward)))

    pieces = sent(0, 0, 0) + [(None, 0, 0, 1, 0, n)] + kept(0, 1, 0) + [(None, 0, 0, 1, 1, n)]
    outgoing, message = pack(side, maps, pieces, (n + 1, n + 1), ids=ids)
    early = exchange(outgoing)
    halo(message)
    got[0] = (early, 0)

    pieces = [(0, 0, 0, n, 0, 0), (0, n, 0, 1, 0, 2 * n)] + kept(1, 0, n, 1) + sent(1, 1, 0, 1)
    for g in range(2, GROUPS):
        pieces += sent(g, 2, (g - 2) * n, 1)
    message, outgoing, later = pack(
        side, [early] + maps, pieces, (2 * n + 1, n, (GROUPS - 2) * n), after=halos[0]
    )
    halo(message)
    got[1] = (exchange(outgoing), 0)
    later = exchange(later)
    for g in range(2, GROUPS):
        got[g] = (later, (g - 2) * n)

    def following(group, after):
        source, begin = got[group]
        pieces = [(0, begin, 0, n, 0, 0)]
        if group + 1 < GROUPS:
            pieces += kept(group + 1, 0, n, 1)
        (message,) = pack(side, [source] + maps, pieces, (sum(p[3] for p in pieces),), after=after)
        return message

    region_float = (ids + 1).astype(jnp.float32)[None]
    groups = [[k * 2 * parts + j for j in range(2 * parts)] for k in range(slabs // 2)]
    held, exchanged, results = (), [], []
    message = following(1, halos[1])
    for group in range(GROUPS):
        if 0 < group < GROUPS - 1:
            message = following(group + 1, tuple(exchanged[1:2]) if group + 2 == GROUPS else ())
        if group < GROUPS - 1:
            halo(message)
        after = (message,) if group + 2 < GROUPS else tuple(results[-1:])
        (lo_kept, hi_kept), (lo_got, hi_got) = halos[group], halos[group + 1]
        before = n if group else 0
        (lo_a, hi_a), (lo_b, hi_b) = halos[0], halos[1]
        pieces = [
            (lo_a, n, 0, 0, False, 0),
            (hi_a, n, 0, 2, False, 0),
            (lo_b, 2 * n, 0, 0, True, 0),
            (hi_b, 2 * n, 0, 2, True, 0),
            (region_float, 0, 0, 1, False, 0),
            (early, n, 0, 1, True, 0),
            (lo_kept, before, n, 0, False, 0),
            (hi_kept, before, n, 2, False, 0),
            (maps[0], (group * width, half), width, 1, False, 0),
            (maps[1], (group * width, half), width, 1, False, width),
            (got[group][0], got[group][1], n, 1, True, 0),
            (lo_got, 0, n, 0, True, 0),
            (hi_got, 0, n, 2, True, 0),
        ]
        direct = group == GROUPS - 1
        moved = list(factors(parts, n, rows, per, direct, side, scal, region_cond, pieces, after))
        if direct:
            for k in [*range(parts, 2 * parts), *range(1, parts)]:
                pairs = [
                    (i * parts + j, (i ^ (k // parts)) * parts + (j ^ (k % parts)))
                    for i in range(slabs)
                    for j in range(parts)
                ]
                moved[k] = lax.ppermute(moved[k], ("slab", "col"), pairs)
        else:
            results += moved
            if exchanged:
                moved[0], exchanged[-1] = lax.optimization_barrier((moved[0], exchanged[-1]))
            moved = [
                lax.all_to_all(
                    moved[0],
                    ("slab", "col"),
                    split_axis=0,
                    concat_axis=0,
                    axis_index_groups=groups,
                    tiled=True,
                )
            ]
            exchanged += moved
        held = place(side, parts, group * width, width, half, moved, held)

    ctrl, obsv = (x.reshape(ADI, parts * col_local, per, rows // parts, lanes) for x in held)
    partial_value = gram(ctrl, obsv)
    count = partial_value.shape[0]
    tiles = partial_value.reshape(slabs, count // slabs, parts, count // parts).transpose(0, 2, 1, 3)
    tiles = tiles.reshape(slabs * parts, count // slabs, count // parts)
    tiles = lax.all_to_all(tiles, ("slab", "col"), split_axis=0, concat_axis=0, tiled=True)
    norm_scale = 1.0 / math.sqrt(total_x * rows * lanes)
    return (ctrl, obsv, jnp.sum(tiles, 0) * norm_scale)


def solution(mesh):
    placed = (
        P("col", "slab", None, None),
        P("col", "slab", None, None),
        P("slab", None, None),
        P(),
        P(),
    )
    return jax.shard_map(
        body,
        mesh=mesh,
        in_specs=placed,
        out_specs=(
            P(None, None, "slab", "col", None),
            P(None, None, "slab", "col", None),
            P("slab", "col"),
        ),
        check_vma=False,
    )
```
